32 devices in a mesh: seq: 16 (over z, y, core), mp: 2 (over x).
Axes of the slice: x: 2, y: 2, z: 4, core: 2. Of those that a mesh axis runs over, the one named last changes fastest.
Arguments:
- tokens: bfloat16 [4096, 1024], P(('seq', 'mp')), may hold values from -6 to 6
- positions: int32 [4096], P('seq'), may hold values from 0 to 1023, as said below
- counts: int32 [16], P('seq'), may hold values from 128 to 256, as said below
- cotangent: bfloat16 [4096, 1024], P(('seq', 'mp')), may hold values from -6 to 6
- gains: bfloat16 [2, 1024], P(None, ('seq', 'mp')), may hold values from 0.5 to 1.5
- in_w: bfloat16 [1024, 3, 1024], P('seq', None, 'mp'), may hold values from -0.1875 to 0.1875
- out_w: bfloat16 [1024, 1024], P('mp', 'seq'), may hold values from -0.1875 to 0.1875
- gate_up: bfloat16 [1024, 2, 4608], P('seq', None, 'mp'), may hold values from -0.1875 to 0.1875
- down_w: bfloat16 [4608, 1024], P('mp', 'seq'), may hold values from -0.09375 to 0.09375
- conv_w: bfloat16 [3, 1024], P(None, ('mp', 'seq')), may hold values from -3 to 3
Outputs:
- mixed: bfloat16 [4096, 1024], P(('seq', 'mp'))
- grad_input: bfloat16 [4096, 1024], P(('seq', 'mp'))
- grad_gains: float32 [2, 1024], P(None, ('seq', 'mp'))
- grad_in_w: float32 [1024, 3, 1024], P('seq', None, 'mp')
- grad_out_w: float32 [1024, 1024], P('mp', 'seq')
- grad_gate_up: float32 [1024, 2, 4608], P('seq', None, 'mp')
- grad_down_w: float32 [4608, 1024], P('mp', 'seq')
- grad_conv_w: float32 [3, 1024], P(None, ('mp', 'seq'))
The draws below stay inside these ranges and needn't reach their ends.
Inputs may be any that keep to these rules, and one draw needn't show every extreme that they name: `counts`: each seq shard's valid rows come first; one shard has 256 valid rows and one has 128. `positions`: on valid rows, the position counts tokens since the document's first token along the token stream; 0 marks a document start and every invalid row. A document has at most 1024 tokens.
All inputs are finite; a program needn't handle non-finite values.
Results may differ from the reference program's by a relative error of at most 0.019.
Values may be sent and summed in bfloat16 or wider, within the bound.
A program may use at most 128 MiB of HBM per device.

```python
import math
import jax
import jax.numpy as jnp
from jax import lax

D = 1024
FF = 4608
GROUP_TOKENS = 256
SHARDS = 16
TOKENS = 4096


def shard_counts(key):
    key = jax.random.fold_in(key, 101)
    first_key, second_key = jax.random.split(key)
    base = jax.random.randint(first_key, (SHARDS,), GROUP_TOKENS // 2, GROUP_TOKENS + 1).astype(jnp.int32)
    order = jax.random.permutation(second_key, SHARDS)
    base = base.at[order[0]].set(GROUP_TOKENS)
    return base.at[order[1]].set(GROUP_TOKENS // 2)


def draw_counts(key, part):
    return shard_counts(key)


def draw_positions(key, part):
    limits = shard_counts(key)
    key = jax.random.fold_in(key, 7)
    key_spans, key_pick = jax.random.split(key)
    total_rows = SHARDS * GROUP_TOKENS
    row_ids = jnp.arange(total_rows, dtype=jnp.int32)
    shard = row_ids // GROUP_TOKENS
    local = row_ids % GROUP_TOKENS
    valid = local < jnp.take(limits, shard)
    flags = valid.astype(jnp.int32)
    stream = (jnp.cumsum(flags) - flags).astype(jnp.int32)
    spans = jax.random.randint(key_spans, (total_rows // 64 + 2,), 64, 1024).astype(jnp.int32)
    spans = spans.at[0].set(1024)
    bounds = jnp.minimum(jnp.cumsum(spans), total_rows).astype(jnp.int32)
    marked = jnp.zeros((total_rows + 1,), jnp.int32).at[bounds].set(1)
    marked = marked.at[0].set(1)
    starts = (jnp.take(marked, stream) == 1) & valid
    edge = (local == 0) & (shard > 0)
    moved = jnp.concatenate([jnp.zeros((1,), jnp.bool_), (starts & edge)[:-1]])
    picked = jax.random.randint(key_pick, (SHARDS,), 0, 2) == 1
    forced = (local == 1) & jnp.take(picked, shard) & (stream >= 1024)
    starts = (starts & jnp.logical_not(edge) | moved | forced | (stream == 0) | (stream == 1024)) & valid
    opened = jnp.where(starts, stream, 0)
    latest = lax.cummax(opened, axis=0)
    return jnp.where(valid, stream - latest, 0).astype(jnp.int32)


def spiked(entries, stream_key, source, target, blocks, factor):
    def block_of(dim):
        return (jnp.arange(entries.shape[dim]) // (entries.shape[dim] // blocks)).reshape((-1,) + (1,) * (entries.ndim - 1 - dim))

    one_side = jax.random.permutation(stream_key, blocks)[block_of(target)]
    other_side = (block_of(target) + blocks // 2) % blocks
    return jnp.where((block_of(source) == one_side) | (block_of(source) == other_side), factor * entries, entries)


def block_levels(rng, dims, pieces, low, high):
    def one(axis_at, parts):
        draws = jax.random.uniform(jax.random.fold_in(jax.random.fold_in(rng, 6), axis_at), (parts,), jnp.float32, low / len(pieces), high / len(pieces))
        return jnp.repeat(jnp.exp(draws), dims[axis_at] // parts).reshape((-1,) + (1,) * (len(dims) - axis_at - 1))

    factor_of = one(*pieces[0])
    for cut in pieces[1:]:
        factor_of = factor_of * one(*cut)
    return factor_of


def scatter_about(own_key, dims, deviation, bound, cuts=(), held_as=jnp.bfloat16):
    values = jax.random.normal(own_key, dims, jnp.float32) * deviation
    if len(cuts) > 0:
        values = block_levels(own_key, dims, cuts, -0.22, 0.18) * values
    return jnp.clip(values, min=-bound, max=bound).astype(held_as)


def heavy_noise(key, shape, scale, reach, shards, heavy, held_as=jnp.bfloat16):
    values = scale * jax.random.normal(key, shape, jnp.float32)
    if shards:
        values = values * block_levels(key, shape, shards, -0.22, 0.18)
    return jnp.clip(spiked(values, jax.random.fold_in(key, 3), *heavy), -reach, reach).astype(held_as)


def setup_inputs(seed: int = 0) -> dict:
    arg_keys = jax.random.split(jax.random.key(seed), 11)
    return {
        "tokens": scatter_about(arg_keys[0], (TOKENS, D), 1.0, 6.0, ((0, 32),)),
        "positions": draw_positions(jax.random.fold_in(arg_keys[10], 71), 0),
        "counts": draw_counts(jax.random.fold_in(arg_keys[10], 71), 0),
        "cotangent": heavy_noise(arg_keys[3], (TOKENS, D), 1.0, 6.0, ((0, 32),), (0, 1, 32, 2.75)),
        "gains": jnp.clip(1.0 + 0.1 * jax.random.normal(arg_keys[4], (2, D), jnp.float32), 0.5, 1.5).astype(jnp.bfloat16),
        "in_w": scatter_about(arg_keys[5], (D, 3, D), D ** -0.5, 0.1875, ((0, 16), (2, 2))),
        "out_w": scatter_about(arg_keys[6], (D, D), D ** -0.5, 0.1875, ((0, 2), (1, 16))),
        "gate_up": scatter_about(arg_keys[7], (D, 2, FF), D ** -0.5, 0.1875, ((0, 16), (2, 2))),
        "down_w": scatter_about(arg_keys[8], (FF, D), FF ** -0.5, 0.09375, ((0, 2), (1, 16))),
        "conv_w": scatter_about(arg_keys[9], (3, D), 0.6, 3.0, ((1, 32),)),
    }


eps = 1e-05
highest = lax.Precision.HIGHEST

@jax.custom_vjp
def low(v):
    return lax.optimization_barrier(v.astype(jnp.bfloat16)).astype(jnp.float32)

@jax.custom_vjp
def low_back(v):
    return v

def low_keep(v):
    return (low(v), None)

def low_pass(kept, grad):
    return (grad,)

def back_keep(v):
    return (v, None)

def back_low(kept, grad):
    return (low(grad),)
low.defvjp(low_keep, low_pass)
low_back.defvjp(back_keep, back_low)

def normed(values, gain):
    return values * lax.rsqrt(lax.optimization_barrier(jnp.mean(values * values, axis=-1, keepdims=True)) + eps) * gain

def feed_forward(resid, gains, gate_up, down_w):
    second = low(normed(resid, gains[1]))
    both = low_back(jnp.dot(second, gate_up.reshape(D, 2 * FF), precision=highest))
    gate = both[:, :FF]
    upper = both[:, FF:]
    hidden = low(jax.nn.silu(gate) * upper)
    return resid + jnp.dot(hidden, down_w, precision=highest)

def forward(tokens, gains, in_w, out_w, gate_up, down_w, conv_w, prev_one, prev_two, keep_one, keep_two, valid):
    first = low(normed(tokens, gains[0]))
    proj = low_back(jnp.dot(first, in_w.reshape(D, 3 * D), precision=highest))
    bgate = proj[:, :D]
    cgate = proj[:, D:2 * D]
    xin = proj[:, 2 * D:]
    gated = low(bgate * xin)
    conv = conv_w[2] * gated + keep_one * conv_w[1] * jnp.take(gated, prev_one, axis=0) + keep_two * conv_w[0] * jnp.take(gated, prev_two, axis=0)
    mixed_in = low(cgate * conv)
    resid = tokens + low_back(jnp.dot(mixed_in, out_w, precision=highest))
    block = math.gcd(TOKENS, 4096)
    stepper = jax.checkpoint(lambda rows_in: feed_forward(rows_in, gains, gate_up, down_w))
    result = lax.map(stepper, resid.reshape(TOKENS // block, block, D)).reshape(TOKENS, D)
    return jnp.where(valid, result, jnp.zeros_like(result))

def reference(tokens, positions, counts, cotangent, gains, in_w, out_w, gate_up, down_w, conv_w):
    row_ids = jnp.arange(TOKENS, dtype=jnp.int32)
    shard = row_ids // GROUP_TOKENS
    local = row_ids % GROUP_TOKENS
    before = jnp.take(counts, jnp.maximum(shard - 1, 0)).astype(jnp.int32)
    edge = (shard - 1) * GROUP_TOKENS + before
    prev_one = jnp.where(local >= 1, row_ids - 1, edge - 1)
    prev_two = jnp.where(local >= 2, row_ids - 2, jnp.where(local == 1, edge - 1, edge - 2))
    prev_one = jnp.clip(prev_one, 0, TOKENS - 1).astype(jnp.int32)
    prev_two = jnp.clip(prev_two, 0, TOKENS - 1).astype(jnp.int32)
    keep_one = (positions >= 1).astype(jnp.float32)[:, None]
    keep_two = (positions >= 2).astype(jnp.float32)[:, None]
    valid = (local < jnp.take(counts, shard))[:, None]

    def wrapped(x_in, g_in, w_in, w_out, w_gu, w_down, w_conv):
        return forward(x_in, g_in, w_in, w_out, w_gu, w_down, w_conv, prev_one, prev_two, keep_one, keep_two, valid)
    result, pullback = jax.vjp(wrapped, tokens.astype(jnp.float32), gains.astype(jnp.float32), in_w.astype(jnp.float32), out_w.astype(jnp.float32), gate_up.astype(jnp.float32), down_w.astype(jnp.float32), conv_w.astype(jnp.float32))
    grads = pullback(cotangent.astype(jnp.float32))
    return (result.astype(jnp.bfloat16), grads[0].astype(jnp.bfloat16), grads[1], grads[2], grads[3], grads[4], grads[5], grads[6])
```

```python
import functools

import jax
import jax.numpy as jnp
from jax import lax
from jax.experimental import pallas as pl
from jax.experimental.pallas import tpu as pltpu
from jax.sharding import PartitionSpec as P

eps = 1e-05
MESH = pl.DeviceIdType.MESH
DEPTH = 4
CORES = 2
LANES = 128
VMEM_BYTES = 58 * 1024 * 1024


def contract_rows(left, right):
    return lax.dot_general(
        left, right, (((0,), (0,)), ((), ())), preferred_element_type=jnp.float32
    )


def contract_cols(left, right):
    return lax.dot_general(
        left, right, (((1,), (1,)), ((), ())), preferred_element_type=jnp.float32
    )


def norm_scale(values):
    return lax.rsqrt(jnp.mean(values * values, axis=-1, keepdims=True) + eps)


def norm_back(values, scale, gain, grad):
    weighted = grad * gain
    cubed = scale * scale * scale
    return scale * weighted - values * cubed * jnp.mean(weighted * values, axis=-1, keepdims=True)


def from_behind(value, axis, steps):
    count = lax.axis_size(axis)
    leading, last = (max(0, -steps), min(count, count - steps))
    return lax.ppermute(value, axis, [(source, source + steps) for source in range(leading, last)])


def pieces_of(widths, size):
    pieces = []
    for place, width in enumerate(widths):
        step = size if width % size == 0 else width
        pieces.extend((place, start, step) for start in range(0, width, step))
    return pieces


def seq_place(tall):
    here = lax.axis_index("seq")
    core = lax.rem(here, CORES)
    chip = here // CORES
    return chip // tall, lax.rem(chip, tall), core


def seq_index(tall, z, y, core):
    return (z * tall + y) * CORES + core


def greet(partners):
    barrier = pltpu.get_barrier_semaphore()
    for partner in partners:
        pl.semaphore_signal(barrier, inc=1, device_id=partner, device_id_type=MESH)
    pl.semaphore_wait(barrier, len(partners))


def remote(source, target, send, recv, partner):
    return pltpu.make_async_remote_copy(
        src_ref=source,
        dst_ref=target,
        send_sem=send,
        recv_sem=recv,
        device_id=partner,
        device_id_type=MESH,
    )


def gather_kernel(pieces, arrays, halves, tall, wide, *refs):
    ins = refs[:arrays]
    rows_in = refs[arrays : arrays + halves]
    outs = refs[arrays + halves : 2 * arrays + halves]
    rows_out = refs[2 * arrays + halves : 2 * (arrays + halves)]
    (own_sem, z_send, z_recv, y_send, y_recv, c_send, c_recv, x_send, x_recv) = refs[
        2 * (arrays + halves) :
    ]
    z, y, core = seq_place(tall)
    part = lax.axis_index("mp")

    def at_z(step):
        return lax.rem(z + step + DEPTH, DEPTH)

    def at_y(step):
        return lax.rem(y + step + tall, tall)

    other_core = {"seq": seq_index(tall, z, y, 1 - core)}
    z_partners = {k: {"seq": seq_index(tall, at_z(k), y, core)} for k in range(1, DEPTH)}
    y_partners = {j: {"seq": seq_index(tall, z, at_y(j), core)} for j in range(1, tall)}
    x_partners = {i: {"mp": lax.rem(part + i, wide)} for i in range(1, wide)}
    greet(
        [other_core, *z_partners.values(), *y_partners.values(), *x_partners.values()]
    )

    def slot(piece, zz, yy, cc):
        place, start, width = pieces[piece]
        return outs[place].at[zz, yy, cc, :, pl.ds(start, width)]

    def own(piece):
        place, start, width = pieces[piece]
        return ins[place].at[:, pl.ds(start, width)]

    waits = []

    def begin(copy):
        copy.start()
        waits.append(copy)

    def send_y(piece, k):
        source = own(piece) if k == 0 else slot(piece, at_z(-k), y, core)
        for j in range(1, tall):
            begin(
                remote(
                    source,
                    slot(piece, at_z(-k), y, core),
                    y_send.at[piece, k, j],
                    y_recv.at[piece, k, j],
                    y_partners[j],
                )
            )

    def send_core(piece, k, j):
        target = slot(piece, at_z(-k), at_y(-j), core)
        source = own(piece) if k == 0 and j == 0 else target
        begin(
            remote(
                source, target, c_send.at[piece, k, j], c_recv.at[piece, k, j], other_core
            )
        )

    for piece in range(len(pieces)):
        for k in range(1, DEPTH):
            begin(
                remote(
                    own(piece),
                    slot(piece, z, y, core),
                    z_send.at[piece, k],
                    z_recv.at[piece, k],
                    z_partners[k],
                )
            )
        send_y(piece, 0)
        if piece == 0:
            for index in range(halves):
                for i in range(1, wide):
                    begin(
                        remote(
                            rows_in[index],
                            rows_out[index].at[part],
                            x_send.at[index, i],
                            x_recv.at[index, i],
                            x_partners[i],
                        )
                    )
    locals_ = []
    for place in range(arrays):
        copy = pltpu.make_async_copy(
            ins[place], outs[place].at[z, y, core], own_sem.at[place]
        )
        copy.start()
        locals_.append(copy)
    for index in range(halves):
        copy = pltpu.make_async_copy(
            rows_in[index], rows_out[index].at[part], own_sem.at[arrays + index]
        )
        copy.start()
        locals_.append(copy)
    for piece in range(len(pieces)):
        send_core(piece, 0, 0)

    def from_z(piece):
        for k in range(1, DEPTH):
            landed = slot(piece, at_z(-k), y, core)
            remote(
                landed, landed, z_send.at[piece, k], z_recv.at[piece, k], z_partners[k]
            ).wait_recv()
            send_y(piece, k)
            send_core(piece, k, 0)

    def from_y(piece):
        for k in range(DEPTH):
            for j in range(1, tall):
                landed = slot(piece, at_z(-k), at_y(-j), core)
                remote(
                    landed,
                    landed,
                    y_send.at[piece, k, j],
                    y_recv.at[piece, k, j],
                    y_partners[j],
                ).wait_recv()
                send_core(piece, k, j)

    for piece in range(len(pieces) + 1):
        if piece < len(pieces):
            from_z(piece)
        if piece > 0:
            from_y(piece - 1)
    for piece in range(len(pieces)):
        for k in range(DEPTH):
            for j in range(tall):
                landed = slot(piece, at_z(-k), at_y(-j), 1 - core)
                remote(
                    landed,
                    landed,
                    c_send.at[piece, k, j],
                    c_recv.at[piece, k, j],
                    other_core,
                ).wait_recv()
    for index in range(halves):
        for i in range(1, wide):
            landed = rows_out[index].at[lax.rem(part - i + wide, wide)]
            remote(
                landed, landed, x_send.at[index, i], x_recv.at[index, i], x_partners[i]
            ).wait_recv()
    for copy in waits:
        copy.wait_send()
    for copy in locals_:
        copy.wait()


def gather_all(shards, row_parts, seq, wide):
    tall = seq // (DEPTH * CORES)
    pieces = pieces_of([shard.shape[1] for shard in shards], 1536)
    count = len(pieces)
    moved = sum(shard.size * shard.dtype.itemsize for shard in shards) * seq
    dma = pltpu.SemaphoreType.DMA
    halves = len(row_parts)
    results = pl.pallas_call(
        functools.partial(gather_kernel, pieces, len(shards), halves, tall, wide),
        out_shape=[
            jax.ShapeDtypeStruct((DEPTH, tall, CORES) + shard.shape, shard.dtype)
            for shard in shards
        ]
        + [jax.ShapeDtypeStruct((wide,) + part.shape, part.dtype) for part in row_parts],
        in_specs=[pl.BlockSpec(memory_space=pl.ANY)] * (len(shards) + halves),
        out_specs=[pl.BlockSpec(memory_space=pl.ANY)] * (len(shards) + halves),
        scratch_shapes=[
            dma((len(shards) + halves,)),
            dma((count, DEPTH)),
            dma((count, DEPTH)),
            dma((count, DEPTH, tall)),
            dma((count, DEPTH, tall)),
            dma((count, DEPTH, tall)),
            dma((count, DEPTH, tall)),
            dma((halves, wide)),
            dma((halves, wide)),
        ],
        compiler_params=pltpu.CompilerParams(collective_id=0, has_side_effects=True),
        cost_estimate=pl.CostEstimate(flops=0, bytes_accessed=16 * moved, transcendentals=0),
        name="gather_weights",
    )(*shards, *row_parts)
    return results[: len(shards)], results[len(shards) :]


def scatter_kernel(pieces, arrays, tall, *refs):
    ins = refs[:arrays]
    outs = refs[arrays : 2 * arrays]
    rest = refs[2 * arrays :]
    from_core = rest[:arrays]
    from_y = rest[arrays : 2 * arrays]
    summed = rest[2 * arrays : 3 * arrays]
    from_z = rest[3 * arrays : 4 * arrays]
    c_send, c_recv, y_send, y_recv, z_send, z_recv = rest[4 * arrays :]
    z, y, core = seq_place(tall)

    def at_z(step):
        return lax.rem(z + step + DEPTH, DEPTH)

    def at_y(step):
        return lax.rem(y + step + tall, tall)

    other_core = {"seq": seq_index(tall, z, y, 1 - core)}
    z_partners = {k: {"seq": seq_index(tall, at_z(k), y, core)} for k in range(1, DEPTH)}
    y_partners = {j: {"seq": seq_index(tall, z, at_y(j), core)} for j in range(1, tall)}
    greet([other_core, *z_partners.values(), *y_partners.values()])

    def core_copy(piece):
        place, start, width = pieces[piece]
        cols = pl.ds(start, width)
        return remote(
            ins[place].at[:, :, 1 - core, :, cols],
            from_core[place].at[:, :, :, cols],
            c_send.at[piece],
            c_recv.at[piece],
            other_core,
        )

    def y_copy(piece, j):
        place, start, width = pieces[piece]
        cols = pl.ds(start, width)
        return remote(
            from_core[place].at[:, at_y(j), :, cols],
            from_y[place].at[j - 1, :, :, cols],
            y_send.at[piece, j],
            y_recv.at[piece, j],
            y_partners[j],
        )

    def z_copy(piece, k):
        place, start, width = pieces[piece]
        cols = pl.ds(start, width)
        return remote(
            summed[place].at[at_z(k), :, cols],
            from_z[place].at[k - 1, :, cols],
            z_send.at[piece, k],
            z_recv.at[piece, k],
            z_partners[k],
        )

    def after_core(piece):
        place, start, width = pieces[piece]
        cols = pl.ds(start, width)
        core_copy(piece).wait_recv()

        def add(block, carry):
            zz = block // tall
            yy = lax.rem(block, tall)
            total = ins[place][zz, yy, core, :, cols].astype(jnp.float32) + from_core[place][
                zz, yy, :, cols
            ].astype(jnp.float32)
            from_core[place][zz, yy, :, cols] = total.astype(from_core[place].dtype)
            return carry

        lax.fori_loop(0, DEPTH * tall, add, 0)
        for j in range(1, tall):
            y_copy(piece, j).start()

    def after_y(piece):
        place, start, width = pieces[piece]
        cols = pl.ds(start, width)
        for j in range(1, tall):
            y_copy(piece, j).wait_recv()

        def add(zz, carry):
            total = from_core[place][zz, y, :, cols].astype(jnp.float32)
            for j in range(1, tall):
                total = total + from_y[place][j - 1, zz, :, cols].astype(jnp.float32)
            summed[place][zz, :, cols] = total.astype(summed[place].dtype)
            return carry

        lax.fori_loop(0, DEPTH, add, 0)
        for k in range(1, DEPTH):
            z_copy(piece, k).start()

    def after_z(piece):
        place, start, width = pieces[piece]
        cols = pl.ds(start, width)
        for k in range(1, DEPTH):
            z_copy(piece, k).wait_recv()
        total = summed[place][z, :, cols].astype(jnp.float32)
        for k in range(1, DEPTH):
            total = total + from_z[place][k - 1, :, cols].astype(jnp.float32)
        outs[place][:, cols] = total

    count = len(pieces)
    for piece in range(count):
        core_copy(piece).start()
    for piece in range(count + 4):
        if piece < count:
            after_core(piece)
        if 2 <= piece < count + 2:
            after_y(piece - 2)
        if 4 <= piece:
            after_z(piece - 4)
    for piece in range(count):
        core_copy(piece).wait_send()
        for j in range(1, tall):
            y_copy(piece, j).wait_send()
        for k in range(1, DEPTH):
            z_copy(piece, k).wait_send()


def scatter_all(terms, seq):
    tall = seq // (DEPTH * CORES)
    terms = [
        term.reshape((DEPTH, tall, CORES, term.shape[0] // seq, term.shape[1])) for term in terms
    ]
    blocks = [term.shape[3:] for term in terms]
    kinds = [term.dtype for term in terms]
    pieces = pieces_of([block[1] for block in blocks], 768)
    count = len(pieces)
    pairs = list(zip(blocks, kinds))
    dma = pltpu.SemaphoreType.DMA
    return pl.pallas_call(
        functools.partial(scatter_kernel, pieces, len(terms), tall),
        out_shape=[jax.ShapeDtypeStruct(block, jnp.float32) for block in blocks],
        in_specs=[pl.BlockSpec(memory_space=pltpu.VMEM)] * len(terms),
        out_specs=[pl.BlockSpec(memory_space=pltpu.VMEM)] * len(terms),
        scratch_shapes=[pltpu.VMEM((DEPTH, tall) + block, kind) for block, kind in pairs]
        + [pltpu.VMEM((max(1, tall - 1), DEPTH) + block, kind) for block, kind in pairs]
        + [pltpu.VMEM((DEPTH,) + block, kind) for block, kind in pairs]
        + [pltpu.VMEM((DEPTH - 1,) + block, kind) for block, kind in pairs]
        + [
            dma((count,)),
            dma((count,)),
            dma((count, tall)),
            dma((count, tall)),
            dma((count, DEPTH)),
            dma((count, DEPTH)),
        ],
        compiler_params=pltpu.CompilerParams(
            collective_id=1, has_side_effects=True, vmem_limit_bytes=VMEM_BYTES
        ),
        name="scatter_grads",
    )(*terms)


def mp_gather(value, axis):
    if lax.axis_size("mp") != 2:
        return lax.all_gather(value, "mp", axis=axis, tiled=True)
    other = lax.ppermute(value, "mp", [(0, 1), (1, 0)])
    first = lax.axis_index("mp") == 0
    return jnp.concatenate(
        [jnp.where(first, value, other), jnp.where(first, other, value)], axis=axis
    )


def mp_sum(value):
    if lax.axis_size("mp") != 2:
        return lax.psum(value, "mp")
    other = lax.ppermute(value.astype(jnp.bfloat16), "mp", [(0, 1), (1, 0)])
    return value + other.astype(jnp.float32)


def mp_sum_own(value, rows):
    if lax.axis_size("mp") != 2:
        return lax.psum_scatter(value, "mp", scatter_dimension=0, tiled=True)
    place = lax.axis_index("mp")
    sent = lax.dynamic_slice_in_dim(value, (1 - place) * rows, rows, 0).astype(jnp.bfloat16)
    other = lax.ppermute(sent, "mp", [(0, 1), (1, 0)])
    return lax.dynamic_slice_in_dim(value, place * rows, rows, 0) + other.astype(jnp.float32)


def on_device(tokens, positions, counts, cotangent, gains, in_w, out_w, gate_up, down_w, conv_w):
    rows, width = tokens.shape
    group = positions.shape[0]
    count = counts[0]
    seq = lax.axis_size("seq")
    wide = lax.axis_size("mp")
    mp_place = lax.axis_index("mp")
    depth = in_w.shape[0]
    chans = in_w.shape[2]
    units = gate_up.shape[2]
    gain_cols = width // seq
    tap_cols = chans // seq

    small = jnp.zeros((16, LANES), jnp.bfloat16)
    small = small.at[:2, :gain_cols].set(mp_gather(gains, 1))
    small = small.at[2:5, :tap_cols].set(conv_w)
    gathered, whole_rows = gather_all(
        [
            small,
            in_w.reshape(depth, 3 * chans),
            out_w.T,
            gate_up.reshape(depth, 2 * units),
            down_w.T,
        ],
        [tokens, cotangent],
        seq,
        wide,
    )
    small_all = gathered[0].reshape(seq, 16, LANES).astype(jnp.float32)
    in_flat = gathered[1].reshape(width, 3 * chans)
    out_turned = gathered[2].reshape(width, chans)
    gu_flat = gathered[3].reshape(width, 2 * units)
    down_turned = gathered[4].reshape(width, units)
    gain_all = small_all[:, :2, :gain_cols].transpose(1, 0, 2).reshape(2, width)
    conv_taps = small_all[:, 2:5, :tap_cols].transpose(1, 0, 2).reshape(3, chans)
    inputs = whole_rows[0].reshape(group, width).astype(jnp.float32)
    valid = (jnp.arange(group, dtype=jnp.int32) < count)[:, None]
    grad_all = whole_rows[1].reshape(group, width)
    grad_all = jnp.where(valid, grad_all, jnp.zeros_like(grad_all))

    def own(value):
        return lax.dynamic_slice_in_dim(value, mp_place * rows, rows, 0)

    scale_one = norm_scale(inputs)
    mixer_all = (inputs * scale_one * gain_all[0]).astype(jnp.bfloat16)
    proj = jnp.dot(mixer_all, in_flat, preferred_element_type=jnp.float32)
    bgate = proj[:, :chans]
    cgate = proj[:, chans : 2 * chans]
    xin = proj[:, 2 * chans :]
    gated = (bgate * xin).astype(jnp.bfloat16)
    tail = lax.dynamic_slice_in_dim(gated, count - 2, 2, 0)
    before = from_behind(tail, "seq", 1)
    extended = jnp.concatenate([before, gated], axis=0).astype(jnp.float32)
    one_back = extended[1 : group + 1]
    two_back = extended[:group]
    keep_one = (positions >= 1).astype(jnp.float32)[:, None]
    keep_two = (positions >= 2).astype(jnp.float32)[:, None]
    current = gated.astype(jnp.float32)
    conv = (
        conv_taps[2] * current
        + keep_one * conv_taps[1] * one_back
        + keep_two * conv_taps[0] * two_back
    )
    mixed_in = (cgate * conv).astype(jnp.bfloat16)
    resid = inputs + mp_sum(contract_cols(mixed_in, out_turned))
    scale_two = norm_scale(resid)
    ff_all = (resid * scale_two * gain_all[1]).astype(jnp.bfloat16)
    both = jnp.dot(ff_all, gu_flat, preferred_element_type=jnp.float32)
    gate = both[:, :units]
    upper = both[:, units:]
    sigma = jax.nn.sigmoid(gate)
    active = gate * sigma
    hidden = (active * upper).astype(jnp.bfloat16)
    final = own(resid) + mp_sum_own(contract_cols(hidden, down_turned), rows)
    mixed = jnp.where(own(valid), final, jnp.zeros_like(final)).astype(jnp.bfloat16)

    grad_hidden = jnp.dot(grad_all, down_turned, preferred_element_type=jnp.float32)
    slope = sigma * (1.0 + gate * (1.0 - sigma))
    grad_both = jnp.concatenate([grad_hidden * upper * slope, grad_hidden * active], axis=1).astype(
        jnp.bfloat16
    )
    term_down = contract_rows(grad_all, hidden).astype(jnp.bfloat16)
    term_gu = contract_rows(ff_all, grad_both).astype(jnp.bfloat16)
    back_two = mp_sum(contract_cols(grad_both, gu_flat))
    grad_resid = grad_all.astype(jnp.float32) + norm_back(resid, scale_two, gain_all[1], back_two)
    gain_two = jnp.sum(own(back_two * resid * scale_two), axis=0)
    grad_o_all = grad_resid.astype(jnp.bfloat16)
    term_out = contract_rows(grad_o_all, mixed_in).astype(jnp.bfloat16)
    grad_mix = jnp.dot(grad_o_all, out_turned, preferred_element_type=jnp.float32)
    grad_cgate = grad_mix * conv
    grad_conv = grad_mix * cgate
    lead_one = keep_one * grad_conv
    lead_two = keep_two * grad_conv
    head = jnp.stack(
        [conv_taps[0] * lead_two[0], conv_taps[1] * lead_one[0] + conv_taps[0] * lead_two[1]]
    )
    after = from_behind(head, "seq", -1)
    zero_one = jnp.zeros((1, chans), jnp.float32)
    zero_two = jnp.zeros((2, chans), jnp.float32)
    row_ids = jnp.arange(group, dtype=jnp.int32)[:, None]
    border = jnp.where(row_ids == count - 2, after[:1], jnp.where(row_ids == count - 1, after[1:], 0.0))
    grad_gated = (
        conv_taps[2] * grad_conv
        + conv_taps[1] * jnp.concatenate([lead_one[1:], zero_one], axis=0)
        + conv_taps[0] * jnp.concatenate([lead_two[2:], zero_two], axis=0)
        + border
    )
    term_conv = jnp.stack(
        [
            jnp.sum(lead_two * two_back, axis=0),
            jnp.sum(lead_one * one_back, axis=0),
            jnp.sum(grad_conv * current, axis=0),
        ]
    )
    grad_proj = jnp.concatenate([grad_gated * xin, grad_cgate, grad_gated * bgate], axis=1).astype(
        jnp.bfloat16
    )
    term_in = contract_rows(mixer_all, grad_proj).astype(jnp.bfloat16)
    back_one = mp_sum_own(contract_cols(grad_proj, in_flat), rows)
    own_inputs = own(inputs)
    own_scale = own(scale_one)
    grad_input = (
        own(grad_resid) + norm_back(own_inputs, own_scale, gain_all[0], back_one)
    ).astype(jnp.bfloat16)
    gain_one = jnp.sum(back_one * own_inputs * own_scale, axis=0)
    gain_terms = jnp.stack([gain_one, gain_two]).reshape(2, seq, gain_cols).transpose(1, 0, 2)
    tap_terms = term_conv.reshape(3, seq, tap_cols).transpose(1, 0, 2)
    small_terms = jnp.zeros((seq, 8, LANES), jnp.float32)
    small_terms = small_terms.at[:, :2, :gain_cols].set(gain_terms)
    small_terms = small_terms.at[:, 2:5, :tap_cols].set(tap_terms)
    sum_gu, sum_down, sum_out, sum_in, sum_small = scatter_all(
        [term_gu, term_down, term_out, term_in, small_terms.reshape(seq * 8, LANES)], seq
    )
    grad_gains = lax.psum_scatter(
        sum_small[:2, :gain_cols], "mp", scatter_dimension=1, tiled=True
    ) if wide != 2 else gain_share(sum_small[:2, :gain_cols], mp_place)
    return (
        mixed,
        grad_input,
        grad_gains,
        sum_in.reshape(depth, 3, chans),
        sum_out.T,
        sum_gu.reshape(depth, 2, units),
        sum_down.T,
        sum_small[2:5, :tap_cols],
    )


def gain_share(sums, place):
    cols = sums.shape[1] // 2
    total = sums + lax.ppermute(sums, "mp", [(0, 1), (1, 0)])
    return lax.dynamic_slice_in_dim(total, place * cols, cols, 1)


def solution(mesh):
    placed = (
        P(("seq", "mp"), None),
        P("seq"),
        P("seq"),
        P(("seq", "mp"), None),
        P(None, ("seq", "mp")),
        P("seq", None, "mp"),
        P("mp", "seq"),
        P("seq", None, "mp"),
        P("mp", "seq"),
        P(None, ("mp", "seq")),
    )
    return jax.shard_map(
        on_device,
        mesh=mesh,
        in_specs=placed,
        out_specs=(
            P(("seq", "mp"), None),
            P(("seq", "mp"), None),
            P(None, ("seq", "mp")),
            P("seq", None, "mp"),
            P("mp", "seq"),
            P("seq", None, "mp"),
            P("mp", "seq"),
            P(None, ("mp", "seq")),
        ),
        check_vma=False,
    )
```

```python
import functools

import jax
import jax.numpy as jnp
from jax import lax
from jax.experimental import pallas as pl
from jax.experimental.pallas import tpu as pltpu
from jax.sharding import PartitionSpec as P

eps = 1e-05
MESH = pl.DeviceIdType.MESH
DEPTH = 4
CORES = 2
LANES = 128
VMEM_BYTES = 58 * 1024 * 1024


def contract_rows(left, right):
    return lax.dot_general(
        left, right, (((0,), (0,)), ((), ())), preferred_element_type=jnp.float32
    )


def contract_cols(left, right):
    return lax.dot_general(
        left, right, (((1,), (1,)), ((), ())), preferred_element_type=jnp.float32
    )


def norm_scale(values):
    return lax.rsqrt(jnp.mean(values * values, axis=-1, keepdims=True) + eps)


def norm_back(values, scale, gain, grad):
    weighted = grad * gain
    cubed = scale * scale * scale
    return scale * weighted - values * cubed * jnp.mean(weighted * values, axis=-1, keepdims=True)


def from_behind(value, axis, steps):
    count = lax.axis_size(axis)
    leading, last = (max(0, -steps), min(count, count - steps))
    return lax.ppermute(value, axis, [(source, source + steps) for source in range(leading, last)])


def pieces_of(widths, size):
    pieces = []
    for place, width in enumerate(widths):
        step = size if width % size == 0 else width
        pieces.extend((place, start, step) for start in range(0, width, step))
    return pieces


def seq_place(tall):
    here = lax.axis_index("seq")
    core = lax.rem(here, CORES)
    chip = here // CORES
    return chip // tall, lax.rem(chip, tall), core


def seq_index(tall, z, y, core):
    return (z * tall + y) * CORES + core


def greet(partners):
    barrier = pltpu.get_barrier_semaphore()
    for partner in partners:
        pl.semaphore_signal(barrier, inc=1, device_id=partner, device_id_type=MESH)
    pl.semaphore_wait(barrier, len(partners))


def remote(source, target, send, recv, partner):
    return pltpu.make_async_remote_copy(
        src_ref=source,
        dst_ref=target,
        send_sem=send,
        recv_sem=recv,
        device_id=partner,
        device_id_type=MESH,
    )


def gather_kernel(pieces, arrays, halves, tall, wide, *refs):
    ins = refs[:arrays]
    rows_in = refs[arrays : arrays + halves]
    outs = refs[arrays + halves : 2 * arrays + halves]
    rows_out = refs[2 * arrays + halves : 2 * (arrays + halves)]
    (own_sem, z_send, z_recv, y_send, y_recv, c_send, c_recv, x_send, x_recv) = refs[
        2 * (arrays + halves) :
    ]
    z, y, core = seq_place(tall)
    part = lax.axis_index("mp")

    def at_z(step):
        return lax.rem(z + step + DEPTH, DEPTH)

    def at_y(step):
        return lax.rem(y + step + tall, tall)

    other_core = {"seq": seq_index(tall, z, y, 1 - core)}
    z_partners = {k: {"seq": seq_index(tall, at_z(k), y, core)} for k in range(1, DEPTH)}
    y_partners = {j: {"seq": seq_index(tall, z, at_y(j), core)} for j in range(1, tall)}
    x_partners = {i: {"mp": lax.rem(part + i, wide)} for i in range(1, wide)}
    greet(
        [other_core, *z_partners.values(), *y_partners.values(), *x_partners.values()]
    )

    def slot(piece, zz, yy, cc):
        place, start, width = pieces[piece]
        return outs[place].at[zz, yy, cc, :, pl.ds(start, width)]

    def own(piece):
        place, start, width = pieces[piece]
        return ins[place].at[:, pl.ds(start, width)]

    waits = []

    def begin(copy):
        copy.start()
        waits.append(copy)

    def send_y(piece, k):
        source = own(piece) if k == 0 else slot(piece, at_z(-k), y, core)
        for j in range(1, tall):
            begin(
                remote(
                    source,
                    slot(piece, at_z(-k), y, core),
                    y_send.at[piece, k, j],
                    y_recv.at[piece, k, j],
                    y_partners[j],
                )
            )

    def send_core(piece, k, j):
        target = slot(piece, at_z(-k), at_y(-j), core)
        source = own(piece) if k == 0 and j == 0 else target
        begin(
            remote(
                source, target, c_send.at[piece, k, j], c_recv.at[piece, k, j], other_core
            )
        )

    for piece in range(len(pieces)):
        for k in range(1, DEPTH):
            begin(
                remote(
                    own(piece),
                    slot(piece, z, y, core),
                    z_send.at[piece, k],
                    z_recv.at[piece, k],
                    z_partners[k],
                )
            )
        send_y(piece, 0)
        if piece == 0:
            for index in range(halves):
                for i in range(1, wide):
                    begin(
                        remote(
                            rows_in[index],
                            rows_out[index].at[part],
                            x_send.at[index, i],
                            x_recv.at[index, i],
                            x_partners[i],
                        )
                    )
    locals_ = []
    for place in range(arrays):
        copy = pltpu.make_async_copy(
            ins[place], outs[place].at[z, y, core], own_sem.at[place]
        )
        copy.start()
        locals_.append(copy)
    for index in range(halves):
        copy = pltpu.make_async_copy(
            rows_in[index], rows_out[index].at[part], own_sem.at[arrays + index]
        )
        copy.start()
        locals_.append(copy)
    for piece in range(len(pieces)):
        send_core(piece, 0, 0)

    def from_z(piece):
        for k in range(1, DEPTH):
            landed = slot(piece, at_z(-k), y, core)
            remote(
                landed, landed, z_send.at[piece, k], z_recv.at[piece, k], z_partners[k]
            ).wait_recv()
            send_y(piece, k)
            send_core(piece, k, 0)

    def from_y(piece):
        for k in range(DEPTH):
            for j in range(1, tall):
                landed = slot(piece, at_z(-k), at_y(-j), core)
                remote(
                    landed,
                    landed,
                    y_send.at[piece, k, j],
                    y_recv.at[piece, k, j],
                    y_partners[j],
                ).wait_recv()
                send_core(piece, k, j)

    for piece in range(len(pieces) + 1):
        if piece < len(pieces):
            from_z(piece)
        if piece > 0:
            from_y(piece - 1)
    for piece in range(len(pieces)):
        for k in range(DEPTH):
            for j in range(tall):
                landed = slot(piece, at_z(-k), at_y(-j), 1 - core)
                remote(
                    landed,
                    landed,
                    c_send.at[piece, k, j],
                    c_recv.at[piece, k, j],
                    other_core,
                ).wait_recv()
    for index in range(halves):
        for i in range(1, wide):
            landed = rows_out[index].at[lax.rem(part - i + wide, wide)]
            remote(
                landed, landed, x_send.at[index, i], x_recv.at[index, i], x_partners[i]
            ).wait_recv()
    for copy in waits:
        copy.wait_send()
    for copy in locals_:
        copy.wait()


def gather_all(shards, row_parts, seq, wide):
    tall = seq // (DEPTH * CORES)
    pieces = pieces_of([shard.shape[1] for shard in shards], 1536)
    count = len(pieces)
    moved = sum(shard.size * shard.dtype.itemsize for shard in shards) * seq
    dma = pltpu.SemaphoreType.DMA
    halves = len(row_parts)
    results = pl.pallas_call(
        functools.partial(gather_kernel, pieces, len(shards), halves, tall, wide),
        out_shape=[
            jax.ShapeDtypeStruct((DEPTH, tall, CORES) + shard.shape, shard.dtype)
            for shard in shards
        ]
        + [jax.ShapeDtypeStruct((wide,) + part.shape, part.dtype) for part in row_parts],
        in_specs=[pl.BlockSpec(memory_space=pl.ANY)] * (len(shards) + halves),
        out_specs=[pl.BlockSpec(memory_space=pl.ANY)] * (len(shards) + halves),
        scratch_shapes=[
            dma((len(shards) + halves,)),
            dma((count, DEPTH)),
            dma((count, DEPTH)),
            dma((count, DEPTH, tall)),
            dma((count, DEPTH, tall)),
            dma((count, DEPTH, tall)),
            dma((count, DEPTH, tall)),
            dma((halves, wide)),
            dma((halves, wide)),
        ],
        compiler_params=pltpu.CompilerParams(collective_id=0, has_side_effects=True),
        cost_estimate=pl.CostEstimate(flops=0, bytes_accessed=16 * moved, transcendentals=0),
        name="gather_weights",
    )(*shards, *row_parts)
    return results[: len(shards)], results[len(shards) :]


def scatter_kernel(pieces, arrays, tall, *refs):
    ins = refs[:arrays]
    outs = refs[arrays : 2 * arrays]
    rest = refs[2 * arrays :]
    from_core = rest[:arrays]
    from_y = rest[arrays : 2 * arrays]
    summed = rest[2 * arrays : 3 * arrays]
    from_z = rest[3 * arrays : 4 * arrays]
    c_send, c_recv, y_send, y_recv, z_send, z_recv = rest[4 * arrays :]
    z, y, core = seq_place(tall)

    def at_z(step):
        return lax.rem(z + step + DEPTH, DEPTH)

    def at_y(step):
        return lax.rem(y + step + tall, tall)

    other_core = {"seq": seq_index(tall, z, y, 1 - core)}
    z_partners = {k: {"seq": seq_index(tall, at_z(k), y, core)} for k in range(1, DEPTH)}
    y_partners = {j: {"seq": seq_index(tall, z, at_y(j), core)} for j in range(1, tall)}
    greet([other_core, *z_partners.values(), *y_partners.values()])

    def core_copy(piece):
        place, start, width = pieces[piece]
        cols = pl.ds(start, width)
        return remote(
            ins[place].at[:, :, 1 - core, :, cols],
            from_core[place].at[:, :, :, cols],
            c_send.at[piece],
            c_recv.at[piece],
            other_core,
        )

    def y_copy(piece, j):
        place, start, width = pieces[piece]
        cols = pl.ds(start, width)
        return remote(
            from_core[place].at[:, at_y(j), :, cols],
            from_y[place].at[j - 1, :, :, cols],
            y_send.at[piece, j],
            y_recv.at[piece, j],
            y_partners[j],
        )

    def z_copy(piece, k):
        place, start, width = pieces[piece]
        cols = pl.ds(start, width)
        return remote(
            summed[place].at[at_z(k), :, cols],
            from_z[place].at[k - 1, :, cols],
            z_send.at[piece, k],
            z_recv.at[piece, k],
            z_partners[k],
        )

    def after_core(piece):
        place, start, width = pieces[piece]
        cols = pl.ds(start, width)
        core_copy(piece).wait_recv()

        def add(block, carry):
            zz = block // tall
            yy = lax.rem(block, tall)
            total = ins[place][zz, yy, core, :, cols].astype(jnp.float32) + from_core[place][
                zz, yy, :, cols
            ].astype(jnp.float32)
            from_core[place][zz, yy, :, cols] = total.astype(from_core[place].dtype)
            return carry

        lax.fori_loop(0, DEPTH * tall, add, 0)
        for j in range(1, tall):
            y_copy(piece, j).start()

    def after_y(piece):
        place, start, width = pieces[piece]
        cols = pl.ds(start, width)
        for j in range(1, tall):
            y_copy(piece, j).wait_recv()

        def add(zz, carry):
            total = from_core[place][zz, y, :, cols].astype(jnp.float32)
            for j in range(1, tall):
                total = total + from_y[place][j - 1, zz, :, cols].astype(jnp.float32)
            summed[place][zz, :, cols] = total.astype(summed[place].dtype)
            return carry

        lax.fori_loop(0, DEPTH, add, 0)
        for k in range(1, DEPTH):
            z_copy(piece, k).start()

    def after_z(piece):
        place, start, width = pieces[piece]
        cols = pl.ds(start, width)
        for k in range(1, DEPTH):
            z_copy(piece, k).wait_recv()
        total = summed[place][z, :, cols].astype(jnp.float32)
        for k in range(1, DEPTH):
            total = total + from_z[place][k - 1, :, cols].astype(jnp.float32)
        outs[place][:, cols] = total

    count = len(pieces)
    for piece in range(count):
        core_copy(piece).start()
    for piece in range(count + 4):
        if piece < count:
            after_core(piece)
        if 2 <= piece < count + 2:
            after_y(piece - 2)
        if 4 <= piece:
            after_z(piece - 4)
    for piece in range(count):
        core_copy(piece).wait_send()
        for j in range(1, tall):
            y_copy(piece, j).wait_send()
        for k in range(1, DEPTH):
            z_copy(piece, k).wait_send()


def scatter_all(terms, seq):
    tall = seq // (DEPTH * CORES)
    terms = [
        term.reshape((DEPTH, tall, CORES, term.shape[0] // seq, term.shape[1])) for term in terms
    ]
    blocks = [term.shape[3:] for term in terms]
    kinds = [term.dtype for term in terms]
    pieces = pieces_of([block[1] for block in blocks], 768)
    count = len(pieces)
    pairs = list(zip(blocks, kinds))
    dma = pltpu.SemaphoreType.DMA
    return pl.pallas_call(
        functools.partial(scatter_kernel, pieces, len(terms), tall),
        out_shape=[jax.ShapeDtypeStruct(block, jnp.float32) for block in blocks],
        in_specs=[pl.BlockSpec(memory_space=pltpu.VMEM)] * len(terms),
        out_specs=[pl.BlockSpec(memory_space=pltpu.VMEM)] * len(terms),
        scratch_shapes=[pltpu.VMEM((DEPTH, tall) + block, kind) for block, kind in pairs]
        + [pltpu.VMEM((max(1, tall - 1), DEPTH) + block, kind) for block, kind in pairs]
        + [pltpu.VMEM((DEPTH,) + block, kind) for block, kind in pairs]
        + [pltpu.VMEM((DEPTH - 1,) + block, kind) for block, kind in pairs]
        + [
            dma((count,)),
            dma((count,)),
            dma((count, tall)),
            dma((count, tall)),
            dma((count, DEPTH)),
            dma((count, DEPTH)),
        ],
        compiler_params=pltpu.CompilerParams(
            collective_id=1, has_side_effects=True, vmem_limit_bytes=VMEM_BYTES
        ),
        name="scatter_grads",
    )(*terms)


def mixer_back_kernel(pieces, ready, *refs):
    (gu_hbm, down_hbm, sent_two, part_two, resid, grad_all, tokens, mixer, mixed_in, conv, cgate, xin,
     bgate, current, one_back, two_back, masks, out_w, in_w, gain, taps) = refs[:21]
    sum_gu, sum_down, sum_out, sum_in, grad_input, small = refs[21:27]
    rest = refs[27:]
    own_gu, own_down, term_out, term_in = rest[:4]
    from_core = rest[4:8]
    from_y = rest[8:12]
    from_z = rest[12:16]
    (recv_two, grad_resid, grad_o, grad_proj, part_one, send_one, recv_one, head, after, lead_one_ref,
     lead_two_ref, gconv_ref, small_send, small_core, small_y, small_z, small_x) = rest[16:33]
    (l_sem, c_send, c_recv, y_send, y_recv, z_send, z_recv, x_send, x_recv, h_sem, s_send, s_recv) = rest[33:]
    outs = (sum_gu, sum_down, sum_out, sum_in)
    terms = (gu_hbm, down_hbm, term_out, term_in)
    tall = 2
    total_seq = DEPTH * tall * CORES
    group = resid.shape[0]
    rows = grad_input.shape[0]
    chans = conv.shape[1]
    z, y, core = seq_place(tall)
    here = lax.axis_index("seq")
    part = lax.axis_index("mp")

    def at_z(step):
        return lax.rem(z + step + DEPTH, DEPTH)

    other_core = {"seq": seq_index(tall, z, y, 1 - core)}
    z_partners = {k: {"seq": seq_index(tall, at_z(k), y, core)} for k in range(1, DEPTH)}
    y_partner = {"seq": seq_index(tall, z, 1 - y, core)}
    x_partner = {"mp": 1 - part}
    earlier = {"seq": lax.rem(here + total_seq - 1, total_seq)}
    later = {"seq": lax.rem(here + 1, total_seq)}
    greet([other_core, *z_partners.values(), y_partner, x_partner, earlier, later])

    def core_copy(piece):
        place, start, width = pieces[piece]
        cols = pl.ds(start, width)
        return remote(terms[place].at[:, :, 1 - core, :, cols], from_core[place].at[:, :, :, cols],
                      c_send.at[piece], c_recv.at[piece], other_core)

    def own_copy(piece):
        place, start, width = pieces[piece]
        cols = pl.ds(start, width)
        return pltpu.make_async_copy(terms[place].at[:, :, core, :, cols],
                                     (own_gu, own_down)[place].at[:, :, :, cols], l_sem.at[piece])

    def y_copy(piece):
        place, start, width = pieces[piece]
        cols = pl.ds(start, width)
        return remote(from_core[place].at[:, 1 - y, :, cols], from_y[place].at[:, :, cols],
                      y_send.at[piece], y_recv.at[piece], y_partner)

    def z_copy(piece, k):
        place, start, width = pieces[piece]
        cols = pl.ds(start, width)
        return remote(from_y[place].at[at_z(k), :, cols], from_z[place].at[k - 1, :, cols],
                      z_send.at[piece, k], z_recv.at[piece, k], z_partners[k])

    def after_core(piece):
        place, start, width = pieces[piece]
        cols = pl.ds(start, width)
        if piece < ready:
            own_copy(piece).wait()
        core_copy(piece).wait_recv()

        def add(block, carry):
            zz = block // tall
            yy = lax.rem(block, tall)
            if place < 2:
                mine = (own_gu, own_down)[place][zz, yy, :, cols]
            else:
                mine = terms[place][zz, yy, core, :, cols]
            total = mine.astype(jnp.float32) + from_core[place][zz, yy, :, cols].astype(jnp.float32)
            from_core[place][zz, yy, :, cols] = total.astype(jnp.bfloat16)
            return carry

        lax.fori_loop(0, DEPTH * tall, add, 0)
        y_copy(piece).start()

    def after_y(piece):
        place, start, width = pieces[piece]
        cols = pl.ds(start, width)
        y_copy(piece).wait_recv()

        def add(zz, carry):
            total = from_core[place][zz, y, :, cols].astype(jnp.float32) + from_y[place][
                zz, :, cols
            ].astype(jnp.float32)
            from_y[place][zz, :, cols] = total.astype(jnp.bfloat16)
            return carry

        lax.fori_loop(0, DEPTH, add, 0)
        for k in range(1, DEPTH):
            z_copy(piece, k).start()

    def after_z(piece):
        place, start, width = pieces[piece]
        cols = pl.ds(start, width)
        for k in range(1, DEPTH):
            z_copy(piece, k).wait_recv()
        total = from_y[place][z, :, cols].astype(jnp.float32)
        for k in range(1, DEPTH):
            total = total + from_z[place][k - 1, :, cols].astype(jnp.float32)
        outs[place][:, cols] = total

    two_copy = remote(sent_two, recv_two, x_send.at[0], x_recv.at[0], x_partner)
    one_copy = remote(send_one, recv_one, x_send.at[1], x_recv.at[1], x_partner)
    head_copy = remote(head, after, h_sem.at[0], h_sem.at[1], earlier)

    count = len(pieces)
    two_copy.start()
    for piece in range(ready):
        core_copy(piece).start()
        own_copy(piece).start()
    for piece in range(ready):
        after_core(piece)

    two_copy.wait_recv()
    gain_two_row = gain[1:2, :]
    step = 32

    def residual(block, acc):
        at = pl.ds(pl.multiple_of(block * step, step), step)
        back = part_two[at, :] + recv_two[at, :].astype(jnp.float32)
        value = resid[at, :]
        scale = norm_scale(value)
        grad = grad_all[at, :].astype(jnp.float32) + norm_back(value, scale, gain_two_row, back)
        grad_resid[at, :] = grad
        grad_o[at, :] = grad.astype(jnp.bfloat16)
        return acc + jnp.sum(back * value * scale, axis=0, keepdims=True)

    gain_two = lax.fori_loop(0, group // step, residual, jnp.zeros((1, resid.shape[1]), jnp.float32))
    small_send[0] = jnp.zeros(small_send.shape[1:], jnp.float32)
    small_send[0, 1:2, :] = gain_two

    keep_one = masks[:, 0:1]
    keep_two = masks[:, 1:2]
    grad_mix = jnp.dot(grad_o[...], out_w[...], preferred_element_type=jnp.float32)
    grad_proj[:, chans : 2 * chans] = (grad_mix * conv[...]).astype(jnp.bfloat16)
    grad_conv = grad_mix * cgate[...]
    lead_one = keep_one * grad_conv
    lead_two = keep_two * grad_conv
    head[...] = jnp.zeros_like(head)
    head[0:1, :] = taps[0:1, :] * lead_two[0:1, :]
    head[1:2, :] = taps[1:2, :] * lead_one[0:1, :] + taps[0:1, :] * lead_two[1:2, :]
    head_copy.start()
    lead_one_ref[...] = lead_one
    lead_two_ref[...] = lead_two
    gconv_ref[...] = grad_conv
    block = group

    def out_block(zz, carry):
        at = pl.ds(pl.multiple_of(zz * block, block), block)
        value = contract_rows(grad_o[:, at], mixed_in[...])
        term_out[zz] = value.astype(jnp.bfloat16).reshape(term_out.shape[1:])
        return carry

    lax.fori_loop(0, DEPTH, out_block, 0)
    out_piece = ready
    core_copy(out_piece).start()
    after_y(0)
    after_y(1)

    head_copy.wait_recv()
    lead_one = lead_one_ref[...]
    lead_two = lead_two_ref[...]
    grad_conv = gconv_ref[...]
    row_ids = lax.broadcasted_iota(jnp.int32, (group, chans), 0)
    moved_one = jnp.where(row_ids < group - 1, pltpu.roll(lead_one, group - 1, 0), 0.0)
    moved_two = jnp.where(row_ids < group - 2, pltpu.roll(lead_two, group - 2, 0), 0.0)
    border = masks[:, 2:3] * after[0:1, :] + masks[:, 3:4] * after[1:2, :]
    border = jnp.where(here == total_seq - 1, jnp.zeros_like(border), border)
    grad_gated = taps[2:3, :] * grad_conv + taps[1:2, :] * moved_one + taps[0:1, :] * moved_two + border
    grad_proj[:, :chans] = (grad_gated * xin[...]).astype(jnp.bfloat16)
    grad_proj[:, 2 * chans :] = (grad_gated * bgate[...]).astype(jnp.bfloat16)
    part_one[...] = contract_cols(grad_proj[...], in_w[...])
    send_one[...] = part_one[pl.ds(pl.multiple_of((1 - part) * rows, rows), rows), :].astype(jnp.bfloat16)
    one_copy.start()

    def in_block(zz, carry):
        at = pl.ds(pl.multiple_of(zz * block, block), block)
        value = contract_rows(mixer[:, at], grad_proj[...])
        term_in[zz] = value.astype(jnp.bfloat16).reshape(term_in.shape[1:])
        return carry

    lax.fori_loop(0, DEPTH, in_block, 0)
    for piece in range(ready + 1, count):
        core_copy(piece).start()
    small_send[0, 2:3, :chans] = jnp.sum(lead_two * two_back[...], axis=0, keepdims=True)
    small_send[0, 3:4, :chans] = jnp.sum(lead_one * one_back[...], axis=0, keepdims=True)
    small_send[0, 4:5, :chans] = jnp.sum(grad_conv * current[...].astype(jnp.float32), axis=0, keepdims=True)
    after_core(ready)
    after_y(2)
    for piece in range(ready + 1, count):
        after_core(piece)
    after_y(3)
    after_z(0)

    one_copy.wait_recv()
    mine = pl.ds(pl.multiple_of(part * rows, rows), rows)
    back_one = part_one[mine, :] + recv_one[...].astype(jnp.float32)
    own_tokens = tokens[mine, :].astype(jnp.float32)
    scale_one = norm_scale(own_tokens)
    grad_input[...] = (
        grad_resid[mine, :] + norm_back(own_tokens, scale_one, gain[0:1, :], back_one)
    ).astype(jnp.bfloat16)
    small_send[0, 0:1, :] = jnp.sum(back_one * own_tokens * scale_one, axis=0, keepdims=True)

    s_core = remote(small_send.at[0], small_core, s_send.at[0], s_recv.at[0], other_core)
    s_y = remote(small_send.at[1], small_y, s_send.at[1], s_recv.at[1], y_partner)
    s_z = [
        remote(small_send.at[2], small_z.at[k - 1], s_send.at[1 + k], s_recv.at[1 + k], z_partners[k])
        for k in range(1, DEPTH)
    ]
    s_x = remote(small_send.at[3], small_x, s_send.at[5], s_recv.at[5], x_partner)
    s_core.start()
    after_y(4)
    after_z(1)
    s_core.wait_recv()
    small_send[1] = small_send[0] + small_core[...]
    s_y.start()
    after_y(5)
    after_z(2)
    s_y.wait_recv()
    small_send[2] = small_send[1] + small_y[...]
    for copy in s_z:
        copy.start()
    after_y(6)
    after_z(3)
    for copy in s_z:
        copy.wait_recv()
    small_send[3] = small_send[2] + small_z[0] + small_z[1] + small_z[2]
    s_x.start()
    for piece in range(7, count):
        after_y(piece)
        after_z(piece - 3)
    s_x.wait_recv()
    first = lax.broadcasted_iota(jnp.int32, small.shape, 0) == 0
    small[...] = small_send[3] + jnp.where(first, small_x[...], 0.0)
    for piece in range(count - 3, count):
        after_z(piece)
    for copy in [two_copy, one_copy, head_copy, s_core, s_y, *s_z, s_x]:
        copy.wait_send()
    for piece in range(count):
        core_copy(piece).wait_send()
        y_copy(piece).wait_send()
        for k in range(1, DEPTH):
            z_copy(piece, k).wait_send()


def mixer_back(term_gu, term_down, values, seq):
    tall = seq // (DEPTH * CORES)
    group, width = values[1].shape
    chans = values[6].shape[1]
    depth = width // seq
    bf, fl = jnp.bfloat16, jnp.float32
    widths = [term_gu.shape[1], term_down.shape[1], chans, 3 * chans]
    pieces = pieces_of(widths, 768)
    ready = sum(1 for piece in pieces if piece[0] < 2)
    count = len(pieces)
    lead = (DEPTH, tall)
    dma = pltpu.SemaphoreType.DMA
    vmem = pltpu.VMEM
    in_vmem = pl.BlockSpec(memory_space=pltpu.VMEM)
    small = (8, width)
    big = [t.reshape((DEPTH, tall, CORES, depth, t.shape[1])) for t in (term_gu, term_down)]
    return pl.pallas_call(
        functools.partial(mixer_back_kernel, pieces, ready),
        out_shape=[jax.ShapeDtypeStruct((depth, w), fl) for w in widths]
        + [jax.ShapeDtypeStruct((group // 2, width), bf), jax.ShapeDtypeStruct(small, fl)],
        in_specs=[pl.BlockSpec(memory_space=pl.ANY)] * 2 + [in_vmem] * len(values),
        out_specs=[in_vmem] * 6,
        scratch_shapes=[vmem(lead + (depth, w), bf) for w in widths[:2]]
        + [vmem(lead + (CORES, depth, w), bf) for w in widths[2:]]
        + [vmem(lead + (depth, w), bf) for w in widths]
        + [vmem((DEPTH, depth, w), bf) for w in widths]
        + [vmem((DEPTH - 1, depth, w), bf) for w in widths]
        + [
            vmem((group, width), bf),
            vmem((group, width), fl),
            vmem((group, width), bf),
            vmem((group, 3 * chans), bf),
            vmem((group, width), fl),
            vmem((group // 2, width), bf),
            vmem((group // 2, width), bf),
            vmem((8, chans), fl),
            vmem((8, chans), fl),
            vmem((group, chans), fl),
            vmem((group, chans), fl),
            vmem((group, chans), fl),
            vmem((4,) + small, fl),
            vmem(small, fl),
            vmem(small, fl),
            vmem((DEPTH - 1,) + small, fl),
            vmem(small, fl),
            dma((count,)),
            dma((count,)),
            dma((count,)),
            dma((count,)),
            dma((count,)),
            dma((count, DEPTH)),
            dma((count, DEPTH)),
            dma((2,)),
            dma((2,)),
            dma((2,)),
            dma((6,)),
            dma((6,)),
        ],
        compiler_params=pltpu.CompilerParams(
            collective_id=2, has_side_effects=True, vmem_limit_bytes=60 * 1024 * 1024
        ),
        name="mixer_backward",
    )(*big, *values)


def mp_gather(value, axis):
    if lax.axis_size("mp") != 2:
        return lax.all_gather(value, "mp", axis=axis, tiled=True)
    other = lax.ppermute(value, "mp", [(0, 1), (1, 0)])
    first = lax.axis_index("mp") == 0
    return jnp.concatenate(
        [jnp.where(first, value, other), jnp.where(first, other, value)], axis=axis
    )


def mp_sum(value):
    if lax.axis_size("mp") != 2:
        return lax.psum(value, "mp")
    other = lax.ppermute(value.astype(jnp.bfloat16), "mp", [(0, 1), (1, 0)])
    return value + other.astype(jnp.float32)


def mp_sum_own(value, rows):
    if lax.axis_size("mp") != 2:
        return lax.psum_scatter(value, "mp", scatter_dimension=0, tiled=True)
    place = lax.axis_index("mp")
    sent = lax.dynamic_slice_in_dim(value, (1 - place) * rows, rows, 0).astype(jnp.bfloat16)
    other = lax.ppermute(sent, "mp", [(0, 1), (1, 0)])
    return lax.dynamic_slice_in_dim(value, place * rows, rows, 0) + other.astype(jnp.float32)


def on_device(tokens, positions, counts, cotangent, gains, in_w, out_w, gate_up, down_w, conv_w):
    rows, width = tokens.shape
    group = positions.shape[0]
    count = counts[0]
    seq = lax.axis_size("seq")
    wide = lax.axis_size("mp")
    mp_place = lax.axis_index("mp")
    depth = in_w.shape[0]
    chans = in_w.shape[2]
    units = gate_up.shape[2]
    gain_cols = width // seq
    tap_cols = chans // seq

    small = jnp.zeros((16, LANES), jnp.bfloat16)
    small = small.at[:2, :gain_cols].set(mp_gather(gains, 1))
    small = small.at[2:5, :tap_cols].set(conv_w)
    gathered, whole_rows = gather_all(
        [
            small,
            in_w.reshape(depth, 3 * chans),
            out_w.T,
            gate_up.reshape(depth, 2 * units),
            down_w.T,
        ],
        [tokens, cotangent],
        seq,
        wide,
    )
    small_all = gathered[0].reshape(seq, 16, LANES).astype(jnp.float32)
    in_flat = gathered[1].reshape(width, 3 * chans)
    out_turned = gathered[2].reshape(width, chans)
    gu_flat = gathered[3].reshape(width, 2 * units)
    down_turned = gathered[4].reshape(width, units)
    gain_all = small_all[:, :2, :gain_cols].transpose(1, 0, 2).reshape(2, width)
    conv_taps = small_all[:, 2:5, :tap_cols].transpose(1, 0, 2).reshape(3, chans)
    inputs = whole_rows[0].reshape(group, width).astype(jnp.float32)
    valid = (jnp.arange(group, dtype=jnp.int32) < count)[:, None]
    grad_all = whole_rows[1].reshape(group, width)
    grad_all = jnp.where(valid, grad_all, jnp.zeros_like(grad_all))

    def own(value):
        return lax.dynamic_slice_in_dim(value, mp_place * rows, rows, 0)

    scale_one = norm_scale(inputs)
    mixer_all = (inputs * scale_one * gain_all[0]).astype(jnp.bfloat16)
    proj = jnp.dot(mixer_all, in_flat, preferred_element_type=jnp.float32)
    bgate = proj[:, :chans]
    cgate = proj[:, chans : 2 * chans]
    xin = proj[:, 2 * chans :]
    gated = (bgate * xin).astype(jnp.bfloat16)
    tail = lax.dynamic_slice_in_dim(gated, count - 2, 2, 0)
    before = from_behind(tail, "seq", 1)
    extended = jnp.concatenate([before, gated], axis=0).astype(jnp.float32)
    one_back = extended[1 : group + 1]
    two_back = extended[:group]
    keep_one = (positions >= 1).astype(jnp.float32)[:, None]
    keep_two = (positions >= 2).astype(jnp.float32)[:, None]
    current = gated.astype(jnp.float32)
    conv = (
        conv_taps[2] * current
        + keep_one * conv_taps[1] * one_back
        + keep_two * conv_taps[0] * two_back
    )
    mixed_in = (cgate * conv).astype(jnp.bfloat16)
    resid = inputs + mp_sum(contract_cols(mixed_in, out_turned))
    scale_two = norm_scale(resid)
    ff_all = (resid * scale_two * gain_all[1]).astype(jnp.bfloat16)
    both = jnp.dot(ff_all, gu_flat, preferred_element_type=jnp.float32)
    gate = both[:, :units]
    upper = both[:, units:]
    sigma = jax.nn.sigmoid(gate)
    active = gate * sigma
    hidden = (active * upper).astype(jnp.bfloat16)
    final = own(resid) + mp_sum_own(contract_cols(hidden, down_turned), rows)
    mixed = jnp.where(own(valid), final, jnp.zeros_like(final)).astype(jnp.bfloat16)

    grad_hidden = jnp.dot(grad_all, down_turned, preferred_element_type=jnp.float32)
    slope = sigma * (1.0 + gate * (1.0 - sigma))
    grad_both = jnp.concatenate([grad_hidden * upper * slope, grad_hidden * active], axis=1).astype(
        jnp.bfloat16
    )
    term_down = contract_rows(grad_all, hidden).astype(jnp.bfloat16)
    term_gu = contract_rows(ff_all, grad_both).astype(jnp.bfloat16)
    partial_two = contract_cols(grad_both, gu_flat)
    if wide == 2 and seq == DEPTH * 2 * CORES:
        row_ids = jnp.arange(group, dtype=jnp.int32)[:, None]
        masks = jnp.concatenate(
            [
                keep_one,
                keep_two,
                (row_ids == count - 2).astype(jnp.float32),
                (row_ids == count - 1).astype(jnp.float32),
            ],
            axis=1,
        )
        sum_gu, sum_down, sum_out, sum_in, grad_input, small_sums = mixer_back(
            term_gu,
            term_down,
            [
                partial_two.astype(jnp.bfloat16),
                partial_two,
                resid,
                grad_all,
                whole_rows[0].reshape(group, width),
                mixer_all,
                mixed_in,
                conv,
                cgate,
                xin,
                bgate,
                gated,
                one_back,
                two_back,
                masks,
                out_turned,
                in_flat,
                gain_all,
                conv_taps,
            ],
            seq,
        )
        here = lax.axis_index("seq")
        gain_size = gains.shape[1]
        return (
            mixed,
            grad_input,
            lax.dynamic_slice(small_sums, (0, (here * wide + mp_place) * gain_size), (2, gain_size)),
            sum_in.reshape(depth, 3, chans),
            sum_out.T,
            sum_gu.reshape(depth, 2, units),
            sum_down.T,
            lax.dynamic_slice(small_sums, (2, here * tap_cols), (3, tap_cols)),
        )
    back_two = mp_sum(partial_two)
    grad_resid = grad_all.astype(jnp.float32) + norm_back(resid, scale_two, gain_all[1], back_two)
    gain_two = jnp.sum(own(back_two * resid * scale_two), axis=0)
    grad_o_all = grad_resid.astype(jnp.bfloat16)
    term_out = contract_rows(grad_o_all, mixed_in).astype(jnp.bfloat16)
    grad_mix = jnp.dot(grad_o_all, out_turned, preferred_element_type=jnp.float32)
    grad_cgate = grad_mix * conv
    grad_conv = grad_mix * cgate
    lead_one = keep_one * grad_conv
    lead_two = keep_two * grad_conv
    head = jnp.stack(
        [conv_taps[0] * lead_two[0], conv_taps[1] * lead_one[0] + conv_taps[0] * lead_two[1]]
    )
    after = from_behind(head, "seq", -1)
    zero_one = jnp.zeros((1, chans), jnp.float32)
    zero_two = jnp.zeros((2, chans), jnp.float32)
    row_ids = jnp.arange(group, dtype=jnp.int32)[:, None]
    border = jnp.where(row_ids == count - 2, after[:1], jnp.where(row_ids == count - 1, after[1:], 0.0))
    grad_gated = (
        conv_taps[2] * grad_conv
        + conv_taps[1] * jnp.concatenate([lead_one[1:], zero_one], axis=0)
        + conv_taps[0] * jnp.concatenate([lead_two[2:], zero_two], axis=0)
        + border
    )
    term_conv = jnp.stack(
        [
            jnp.sum(lead_two * two_back, axis=0),
            jnp.sum(lead_one * one_back, axis=0),
            jnp.sum(grad_conv * current, axis=0),
        ]
    )
    grad_proj = jnp.concatenate([grad_gated * xin, grad_cgate, grad_gated * bgate], axis=1).astype(
        jnp.bfloat16
    )
    term_in = contract_rows(mixer_all, grad_proj).astype(jnp.bfloat16)
    back_one = mp_sum_own(contract_cols(grad_proj, in_flat), rows)
    own_inputs = own(inputs)
    own_scale = own(scale_one)
    grad_input = (
        own(grad_resid) + norm_back(own_inputs, own_scale, gain_all[0], back_one)
    ).astype(jnp.bfloat16)
    gain_one = jnp.sum(back_one * own_inputs * own_scale, axis=0)
    gain_terms = jnp.stack([gain_one, gain_two]).reshape(2, seq, gain_cols).transpose(1, 0, 2)
    tap_terms = term_conv.reshape(3, seq, tap_cols).transpose(1, 0, 2)
    small_terms = jnp.zeros((seq, 8, LANES), jnp.float32)
    small_terms = small_terms.at[:, :2, :gain_cols].set(gain_terms)
    small_terms = small_terms.at[:, 2:5, :tap_cols].set(tap_terms)
    sum_gu, sum_down, sum_out, sum_in, sum_small = scatter_all(
        [term_gu, term_down, term_out, term_in, small_terms.reshape(seq * 8, LANES)], seq
    )
    grad_gains = lax.psum_scatter(
        sum_small[:2, :gain_cols], "mp", scatter_dimension=1, tiled=True
    ) if wide != 2 else gain_share(sum_small[:2, :gain_cols], mp_place)
    return (
        mixed,
        grad_input,
        grad_gains,
        sum_in.reshape(depth, 3, chans),
        sum_out.T,
        sum_gu.reshape(depth, 2, units),
        sum_down.T,
        sum_small[2:5, :tap_cols],
    )


def gain_share(sums, place):
    cols = sums.shape[1] // 2
    total = sums + lax.ppermute(sums, "mp", [(0, 1), (1, 0)])
    return lax.dynamic_slice_in_dim(total, place * cols, cols, 1)


def solution(mesh):
    placed = (
        P(("seq", "mp"), None),
        P("seq"),
        P("seq"),
        P(("seq", "mp"), None),
        P(None, ("seq", "mp")),
        P("seq", None, "mp"),
        P("mp", "seq"),
        P("seq", None, "mp"),
        P("mp", "seq"),
        P(None, ("mp", "seq")),
    )
    return jax.shard_map(
        on_device,
        mesh=mesh,
        in_specs=placed,
        out_specs=(
            P(("seq", "mp"), None),
            P(("seq", "mp"), None),
            P(None, ("seq", "mp")),
            P("seq", None, "mp"),
            P("mp", "seq"),
            P("seq", None, "mp"),
            P("mp", "seq"),
            P(None, ("mp", "seq")),
        ),
        check_vma=False,
    )
```

```python
import functools

import jax
import jax.numpy as jnp
from jax import lax
from jax.experimental import pallas as pl
from jax.experimental.pallas import tpu as pltpu
from jax.sharding import PartitionSpec as P

eps = 1e-05
MESH = pl.DeviceIdType.MESH
DEPTH = 4
CORES = 2
LANES = 128
VMEM_BYTES = 58 * 1024 * 1024


def contract_rows(left, right):
    return lax.dot_general(
        left, right, (((0,), (0,)), ((), ())), preferred_element_type=jnp.float32
    )


def contract_cols(left, right):
    return lax.dot_general(
        left, right, (((1,), (1,)), ((), ())), preferred_element_type=jnp.float32
    )


def norm_scale(values):
    return lax.rsqrt(jnp.mean(values * values, axis=-1, keepdims=True) + eps)


def norm_back(values, scale, gain, grad):
    weighted = grad * gain
    cubed = scale * scale * scale
    return scale * weighted - values * cubed * jnp.mean(weighted * values, axis=-1, keepdims=True)


def from_behind(value, axis, steps):
    count = lax.axis_size(axis)
    leading, last = (max(0, -steps), min(count, count - steps))
    return lax.ppermute(value, axis, [(source, source + steps) for source in range(leading, last)])


def pieces_of(widths, size):
    pieces = []
    for place, width in enumerate(widths):
        step = size if width % size == 0 else width
        pieces.extend((place, start, step) for start in range(0, width, step))
    return pieces


def seq_place(tall):
    here = lax.axis_index("seq")
    core = lax.rem(here, CORES)
    chip = here // CORES
    return chip // tall, lax.rem(chip, tall), core


def seq_index(tall, z, y, core):
    return (z * tall + y) * CORES + core


def greet(partners):
    barrier = pltpu.get_barrier_semaphore()
    for partner in partners:
        pl.semaphore_signal(barrier, inc=1, device_id=partner, device_id_type=MESH)
    pl.semaphore_wait(barrier, len(partners))


def remote(source, target, send, recv, partner):
    return pltpu.make_async_remote_copy(
        src_ref=source,
        dst_ref=target,
        send_sem=send,
        recv_sem=recv,
        device_id=partner,
        device_id_type=MESH,
    )


def gather_kernel(pieces, arrays, halves, tall, wide, *refs):
    ins = refs[:arrays]
    rows_in = refs[arrays : arrays + halves]
    outs = refs[arrays + halves : 2 * arrays + halves]
    rows_out = refs[2 * arrays + halves : 2 * (arrays + halves)]
    (own_sem, z_send, z_recv, y_send, y_recv, c_send, c_recv, x_send, x_recv) = refs[
        2 * (arrays + halves) :
    ]
    z, y, core = seq_place(tall)
    part = lax.axis_index("mp")

    def at_z(step):
        return lax.rem(z + step + DEPTH, DEPTH)

    def at_y(step):
        return lax.rem(y + step + tall, tall)

    other_core = {"seq": seq_index(tall, z, y, 1 - core)}
    z_partners = {k: {"seq": seq_index(tall, at_z(k), y, core)} for k in range(1, DEPTH)}
    y_partners = {j: {"seq": seq_index(tall, z, at_y(j), core)} for j in range(1, tall)}
    x_partners = {i: {"mp": lax.rem(part + i, wide)} for i in range(1, wide)}
    greet(
        [other_core, *z_partners.values(), *y_partners.values(), *x_partners.values()]
    )

    def slot(piece, zz, yy, cc):
        place, start, width = pieces[piece]
        return outs[place].at[zz, yy, cc, :, pl.ds(start, width)]

    def own(piece):
        place, start, width = pieces[piece]
        return ins[place].at[:, pl.ds(start, width)]

    waits = []

    def begin(copy):
        copy.start()
        waits.append(copy)

    def send_y(piece, k):
        source = own(piece) if k == 0 else slot(piece, at_z(-k), y, core)
        for j in range(1, tall):
            begin(
                remote(
                    source,
                    slot(piece, at_z(-k), y, core),
                    y_send.at[piece, k, j],
                    y_recv.at[piece, k, j],
                    y_partners[j],
                )
            )

    def send_core(piece, k, j):
        target = slot(piece, at_z(-k), at_y(-j), core)
        source = own(piece) if k == 0 and j == 0 else target
        begin(
            remote(
                source, target, c_send.at[piece, k, j], c_recv.at[piece, k, j], other_core
            )
        )

    def send_z(piece):
        for k in range(1, DEPTH):
            begin(
                remote(
                    own(piece),
                    slot(piece, z, y, core),
                    z_send.at[piece, k],
                    z_recv.at[piece, k],
                    z_partners[k],
                )
            )

    ahead = 3
    for piece in range(min(ahead, len(pieces))):
        send_z(piece)
    for piece in range(len(pieces)):
        send_y(piece, 0)
        if piece == 0:
            for index in range(halves):
                for i in range(1, wide):
                    begin(
                        remote(
                            rows_in[index],
                            rows_out[index].at[part],
                            x_send.at[index, i],
                            x_recv.at[index, i],
                            x_partners[i],
                        )
                    )
    locals_ = []
    for place in range(arrays):
        copy = pltpu.make_async_copy(
            ins[place], outs[place].at[z, y, core], own_sem.at[place]
        )
        copy.start()
        locals_.append(copy)
    for index in range(halves):
        copy = pltpu.make_async_copy(
            rows_in[index], rows_out[index].at[part], own_sem.at[arrays + index]
        )
        copy.start()
        locals_.append(copy)
    for piece in range(len(pieces)):
        send_core(piece, 0, 0)

    def from_z(piece):
        for k in range(1, DEPTH):
            landed = slot(piece, at_z(-k), y, core)
            remote(
                landed, landed, z_send.at[piece, k], z_recv.at[piece, k], z_partners[k]
            ).wait_recv()
            send_y(piece, k)
            send_core(piece, k, 0)
        if piece + ahead < len(pieces):
            send_z(piece + ahead)

    def from_y(piece):
        for k in range(DEPTH):
            for j in range(1, tall):
                landed = slot(piece, at_z(-k), at_y(-j), core)
                remote(
                    landed,
                    landed,
                    y_send.at[piece, k, j],
                    y_recv.at[piece, k, j],
                    y_partners[j],
                ).wait_recv()
                send_core(piece, k, j)

    for piece in range(len(pieces) + 1):
        if piece < len(pieces):
            from_z(piece)
        if piece > 0:
            from_y(piece - 1)
    for piece in range(len(pieces)):
        for k in range(DEPTH):
            for j in range(tall):
                landed = slot(piece, at_z(-k), at_y(-j), 1 - core)
                remote(
                    landed,
                    landed,
                    c_send.at[piece, k, j],
                    c_recv.at[piece, k, j],
                    other_core,
                ).wait_recv()
    for index in range(halves):
        for i in range(1, wide):
            landed = rows_out[index].at[lax.rem(part - i + wide, wide)]
            remote(
                landed, landed, x_send.at[index, i], x_recv.at[index, i], x_partners[i]
            ).wait_recv()
    for copy in waits:
        copy.wait_send()
    for copy in locals_:
        copy.wait()


def gather_all(shards, row_parts, seq, wide):
    tall = seq // (DEPTH * CORES)
    pieces = pieces_of([shard.shape[1] for shard in shards], 768)
    count = len(pieces)
    moved = sum(shard.size * shard.dtype.itemsize for shard in shards) * seq
    dma = pltpu.SemaphoreType.DMA
    halves = len(row_parts)
    results = pl.pallas_call(
        functools.partial(gather_kernel, pieces, len(shards), halves, tall, wide),
        out_shape=[
            jax.ShapeDtypeStruct((DEPTH, tall, CORES) + shard.shape, shard.dtype)
            for shard in shards
        ]
        + [jax.ShapeDtypeStruct((wide,) + part.shape, part.dtype) for part in row_parts],
        in_specs=[pl.BlockSpec(memory_space=pl.ANY)] * (len(shards) + halves),
        out_specs=[pl.BlockSpec(memory_space=pl.ANY)] * (len(shards) + halves),
        scratch_shapes=[
            dma((len(shards) + halves,)),
            dma((count, DEPTH)),
            dma((count, DEPTH)),
            dma((count, DEPTH, tall)),
            dma((count, DEPTH, tall)),
            dma((count, DEPTH, tall)),
            dma((count, DEPTH, tall)),
            dma((halves, wide)),
            dma((halves, wide)),
        ],
        compiler_params=pltpu.CompilerParams(collective_id=0, has_side_effects=True),
        cost_estimate=pl.CostEstimate(flops=0, bytes_accessed=16 * moved, transcendentals=0),
        name="gather_weights",
    )(*shards, *row_parts)
    return results[: len(shards)], results[len(shards) :]


def scatter_kernel(pieces, arrays, tall, *refs):
    ins = refs[:arrays]
    outs = refs[arrays : 2 * arrays]
    rest = refs[2 * arrays :]
    from_core = rest[:arrays]
    from_y = rest[arrays : 2 * arrays]
    summed = rest[2 * arrays : 3 * arrays]
    from_z = rest[3 * arrays : 4 * arrays]
    c_send, c_recv, y_send, y_recv, z_send, z_recv = rest[4 * arrays :]
    z, y, core = seq_place(tall)

    def at_z(step):
        return lax.rem(z + step + DEPTH, DEPTH)

    def at_y(step):
        return lax.rem(y + step + tall, tall)

    other_core = {"seq": seq_index(tall, z, y, 1 - core)}
    z_partners = {k: {"seq": seq_index(tall, at_z(k), y, core)} for k in range(1, DEPTH)}
    y_partners = {j: {"seq": seq_index(tall, z, at_y(j), core)} for j in range(1, tall)}
    greet([other_core, *z_partners.values(), *y_partners.values()])

    def core_copy(piece):
        place, start, width = pieces[piece]
        cols = pl.ds(start, width)
        return remote(
            ins[place].at[:, :, 1 - core, :, cols],
            from_core[place].at[:, :, :, cols],
            c_send.at[piece],
            c_recv.at[piece],
            other_core,
        )

    def y_copy(piece, j):
        place, start, width = pieces[piece]
        cols = pl.ds(start, width)
        return remote(
            from_core[place].at[:, at_y(j), :, cols],
            from_y[place].at[j - 1, :, :, cols],
            y_send.at[piece, j],
            y_recv.at[piece, j],
            y_partners[j],
        )

    def z_copy(piece, k):
        place, start, width = pieces[piece]
        cols = pl.ds(start, width)
        return remote(
            summed[place].at[at_z(k), :, cols],
            from_z[place].at[k - 1, :, cols],
            z_send.at[piece, k],
            z_recv.at[piece, k],
            z_partners[k],
        )

    def after_core(piece):
        place, start, width = pieces[piece]
        cols = pl.ds(start, width)
        core_copy(piece).wait_recv()

        def add(block, carry):
            zz = block // tall
            yy = lax.rem(block, tall)
            total = ins[place][zz, yy, core, :, cols].astype(jnp.float32) + from_core[place][
                zz, yy, :, cols
            ].astype(jnp.float32)
            from_core[place][zz, yy, :, cols] = total.astype(from_core[place].dtype)
            return carry

        lax.fori_loop(0, DEPTH * tall, add, 0)
        for j in range(1, tall):
            y_copy(piece, j).start()

    def after_y(piece):
        place, start, width = pieces[piece]
        cols = pl.ds(start, width)
        for j in range(1, tall):
            y_copy(piece, j).wait_recv()

        def add(zz, carry):
            total = from_core[place][zz, y, :, cols].astype(jnp.float32)
            for j in range(1, tall):
                total = total + from_y[place][j - 1, zz, :, cols].astype(jnp.float32)
            summed[place][zz, :, cols] = total.astype(summed[place].dtype)
            return carry

        lax.fori_loop(0, DEPTH, add, 0)
        for k in range(1, DEPTH):
            z_copy(piece, k).start()

    def after_z(piece):
        place, start, width = pieces[piece]
        cols = pl.ds(start, width)
        for k in range(1, DEPTH):
            z_copy(piece, k).wait_recv()
        total = summed[place][z, :, cols].astype(jnp.float32)
        for k in range(1, DEPTH):
            total = total + from_z[place][k - 1, :, cols].astype(jnp.float32)
        outs[place][:, cols] = total

    count = len(pieces)
    for piece in range(count):
        core_copy(piece).start()
    for piece in range(count + 4):
        if piece < count:
            after_core(piece)
        if 2 <= piece < count + 2:
            after_y(piece - 2)
        if 4 <= piece:
            after_z(piece - 4)
    for piece in range(count):
        core_copy(piece).wait_send()
        for j in range(1, tall):
            y_copy(piece, j).wait_send()
        for k in range(1, DEPTH):
            z_copy(piece, k).wait_send()


def scatter_all(terms, seq):
    tall = seq // (DEPTH * CORES)
    terms = [
        term.reshape((DEPTH, tall, CORES, term.shape[0] // seq, term.shape[1])) for term in terms
    ]
    blocks = [term.shape[3:] for term in terms]
    kinds = [term.dtype for term in terms]
    pieces = pieces_of([block[1] for block in blocks], 768)
    count = len(pieces)
    pairs = list(zip(blocks, kinds))
    dma = pltpu.SemaphoreType.DMA
    return pl.pallas_call(
        functools.partial(scatter_kernel, pieces, len(terms), tall),
        out_shape=[jax.ShapeDtypeStruct(block, jnp.float32) for block in blocks],
        in_specs=[pl.BlockSpec(memory_space=pltpu.VMEM)] * len(terms),
        out_specs=[pl.BlockSpec(memory_space=pltpu.VMEM)] * len(terms),
        scratch_shapes=[pltpu.VMEM((DEPTH, tall) + block, kind) for block, kind in pairs]
        + [pltpu.VMEM((max(1, tall - 1), DEPTH) + block, kind) for block, kind in pairs]
        + [pltpu.VMEM((DEPTH,) + block, kind) for block, kind in pairs]
        + [pltpu.VMEM((DEPTH - 1,) + block, kind) for block, kind in pairs]
        + [
            dma((count,)),
            dma((count,)),
            dma((count, tall)),
            dma((count, tall)),
            dma((count, DEPTH)),
            dma((count, DEPTH)),
        ],
        compiler_params=pltpu.CompilerParams(
            collective_id=1, has_side_effects=True, vmem_limit_bytes=VMEM_BYTES
        ),
        name="scatter_grads",
    )(*terms)


def mixer_back_kernel(pieces, ready, *refs):
    (gu_hbm, down_hbm, sent_two, part_two, resid, grad_all, tokens, mixer, mixed_in, conv, cgate, xin,
     bgate, current, one_back, two_back, masks, out_w, in_w, gain, taps) = refs[:21]
    sum_gu, sum_down, sum_out, sum_in, grad_input, small = refs[21:27]
    rest = refs[27:]
    own_gu, own_down, term_out, term_in = rest[:4]
    from_core = rest[4:8]
    from_y = rest[8:12]
    from_z = rest[12:16]
    (recv_two, grad_resid, grad_o, grad_proj, part_one, send_one, recv_one, head, after, lead_one_ref,
     lead_two_ref, gconv_ref, small_send, small_core, small_y, small_z, small_x) = rest[16:33]
    (l_sem, c_send, c_recv, y_send, y_recv, z_send, z_recv, x_send, x_recv, h_sem, s_send, s_recv) = rest[33:]
    outs = (sum_gu, sum_down, sum_out, sum_in)
    terms = (gu_hbm, down_hbm, term_out, term_in)
    tall = 2
    total_seq = DEPTH * tall * CORES
    group = resid.shape[0]
    rows = grad_input.shape[0]
    chans = conv.shape[1]
    z, y, core = seq_place(tall)
    here = lax.axis_index("seq")
    part = lax.axis_index("mp")

    def at_z(step):
        return lax.rem(z + step + DEPTH, DEPTH)

    other_core = {"seq": seq_index(tall, z, y, 1 - core)}
    z_partners = {k: {"seq": seq_index(tall, at_z(k), y, core)} for k in range(1, DEPTH)}
    y_partner = {"seq": seq_index(tall, z, 1 - y, core)}
    x_partner = {"mp": 1 - part}
    earlier = {"seq": lax.rem(here + total_seq - 1, total_seq)}
    later = {"seq": lax.rem(here + 1, total_seq)}
    greet([other_core, *z_partners.values(), y_partner, x_partner, earlier, later])

    def core_copy(piece):
        place, start, width = pieces[piece]
        cols = pl.ds(start, width)
        return remote(terms[place].at[:, :, 1 - core, :, cols], from_core[place].at[:, :, :, cols],
                      c_send.at[piece], c_recv.at[piece], other_core)

    def own_copy(piece):
        place, start, width = pieces[piece]
        cols = pl.ds(start, width)
        return pltpu.make_async_copy(terms[place].at[:, :, core, :, cols],
                                     (own_gu, own_down)[place].at[:, :, :, cols], l_sem.at[piece])

    def y_copy(piece):
        place, start, width = pieces[piece]
        cols = pl.ds(start, width)
        return remote(from_core[place].at[:, 1 - y, :, cols], from_y[place].at[:, :, cols],
                      y_send.at[piece], y_recv.at[piece], y_partner)

    def z_copy(piece, k):
        place, start, width = pieces[piece]
        cols = pl.ds(start, width)
        return remote(from_y[place].at[at_z(k), :, cols], from_z[place].at[k - 1, :, cols],
                      z_send.at[piece, k], z_recv.at[piece, k], z_partners[k])

    def after_core(piece):
        place, start, width = pieces[piece]
        cols = pl.ds(start, width)
        if piece < ready:
            own_copy(piece).wait()
        core_copy(piece).wait_recv()

        def add(block, carry):
            zz = block // tall
            yy = lax.rem(block, tall)
            if place < 2:
                mine = (own_gu, own_down)[place][zz, yy, :, cols]
            else:
                mine = terms[place][zz, yy, core, :, cols]
            total = mine.astype(jnp.float32) + from_core[place][zz, yy, :, cols].astype(jnp.float32)
            from_core[place][zz, yy, :, cols] = total.astype(jnp.bfloat16)
            return carry

        lax.fori_loop(0, DEPTH * tall, add, 0)
        y_copy(piece).start()

    def after_y(piece):
        place, start, width = pieces[piece]
        cols = pl.ds(start, width)
        y_copy(piece).wait_recv()

        def add(zz, carry):
            total = from_core[place][zz, y, :, cols].astype(jnp.float32) + from_y[place][
                zz, :, cols
            ].astype(jnp.float32)
            from_y[place][zz, :, cols] = total.astype(jnp.bfloat16)
            return carry

        lax.fori_loop(0, DEPTH, add, 0)
        for k in range(1, DEPTH):
            z_copy(piece, k).start()

    def after_z(piece):
        place, start, width = pieces[piece]
        cols = pl.ds(start, width)
        for k in range(1, DEPTH):
            z_copy(piece, k).wait_recv()
        total = from_y[place][z, :, cols].astype(jnp.float32)
        for k in range(1, DEPTH):
            total = total + from_z[place][k - 1, :, cols].astype(jnp.float32)
        outs[place][:, cols] = total

    two_copy = remote(sent_two, recv_two, x_send.at[0], x_recv.at[0], x_partner)
    one_copy = remote(send_one, recv_one, x_send.at[1], x_recv.at[1], x_partner)
    head_copy = remote(head, after, h_sem.at[0], h_sem.at[1], earlier)

    count = len(pieces)
    ahead = 3

    def begin_core(piece):
        core_copy(piece).start()
        if piece < ready:
            own_copy(piece).start()

    def turn(piece):
        if piece < count:
            after_core(piece)
            if piece + ahead < ready:
                begin_core(piece + ahead)
        if 0 <= piece - 2 < count:
            after_y(piece - 2)
        if 0 <= piece - 4 < count:
            after_z(piece - 4)

    two_copy.start()
    for piece in range(ahead):
        begin_core(piece)
    turn(0)
    turn(1)

    two_copy.wait_recv()
    gain_two_row = gain[1:2, :]
    step = 32

    def residual(block, acc):
        at = pl.ds(pl.multiple_of(block * step, step), step)
        back = part_two[at, :] + recv_two[at, :].astype(jnp.float32)
        value = resid[at, :]
        scale = norm_scale(value)
        grad = grad_all[at, :].astype(jnp.float32) + norm_back(value, scale, gain_two_row, back)
        grad_resid[at, :] = grad
        grad_o[at, :] = grad.astype(jnp.bfloat16)
        return acc + jnp.sum(back * value * scale, axis=0, keepdims=True)

    gain_two = lax.fori_loop(0, group // step, residual, jnp.zeros((1, resid.shape[1]), jnp.float32))
    small_send[0] = jnp.zeros(small_send.shape[1:], jnp.float32)
    small_send[0, 1:2, :] = gain_two

    turn(2)

    keep_one = masks[:, 0:1]
    keep_two = masks[:, 1:2]
    grad_mix = jnp.dot(grad_o[...], out_w[...], preferred_element_type=jnp.float32)
    grad_proj[:, chans : 2 * chans] = (grad_mix * conv[...]).astype(jnp.bfloat16)
    grad_conv = grad_mix * cgate[...]
    lead_one = keep_one * grad_conv
    lead_two = keep_two * grad_conv
    head[...] = jnp.zeros_like(head)
    head[0:1, :] = taps[0:1, :] * lead_two[0:1, :]
    head[1:2, :] = taps[1:2, :] * lead_one[0:1, :] + taps[0:1, :] * lead_two[1:2, :]
    head_copy.start()
    lead_one_ref[...] = lead_one
    lead_two_ref[...] = lead_two
    gconv_ref[...] = grad_conv
    turn(3)
    block = group

    def out_block(zz, carry):
        at = pl.ds(pl.multiple_of(zz * block, block), block)
        value = contract_rows(grad_o[:, at], mixed_in[...])
        term_out[zz] = value.astype(jnp.bfloat16).reshape(term_out.shape[1:])
        return carry

    lax.fori_loop(0, DEPTH, out_block, 0)
    turn(4)
    begin_core(ready)

    head_copy.wait_recv()
    lead_one = lead_one_ref[...]
    lead_two = lead_two_ref[...]
    grad_conv = gconv_ref[...]
    row_ids = lax.broadcasted_iota(jnp.int32, (group, chans), 0)
    moved_one = jnp.where(row_ids < group - 1, pltpu.roll(lead_one, group - 1, 0), 0.0)
    moved_two = jnp.where(row_ids < group - 2, pltpu.roll(lead_two, group - 2, 0), 0.0)
    border = masks[:, 2:3] * after[0:1, :] + masks[:, 3:4] * after[1:2, :]
    border = jnp.where(here == total_seq - 1, jnp.zeros_like(border), border)
    grad_gated = taps[2:3, :] * grad_conv + taps[1:2, :] * moved_one + taps[0:1, :] * moved_two + border
    grad_proj[:, :chans] = (grad_gated * xin[...]).astype(jnp.bfloat16)
    grad_proj[:, 2 * chans :] = (grad_gated * bgate[...]).astype(jnp.bfloat16)
    part_one[...] = contract_cols(grad_proj[...], in_w[...])
    send_one[...] = part_one[pl.ds(pl.multiple_of((1 - part) * rows, rows), rows), :].astype(jnp.bfloat16)
    one_copy.start()

    turn(5)

    def in_block(zz, carry):
        at = pl.ds(pl.multiple_of(zz * block, block), block)
        value = contract_rows(mixer[:, at], grad_proj[...])
        term_in[zz] = value.astype(jnp.bfloat16).reshape(term_in.shape[1:])
        return carry

    lax.fori_loop(0, DEPTH, in_block, 0)
    for piece in range(ready + 1, count):
        begin_core(piece)
    turn(6)
    small_send[0, 2:3, :chans] = jnp.sum(lead_two * two_back[...], axis=0, keepdims=True)
    small_send[0, 3:4, :chans] = jnp.sum(lead_one * one_back[...], axis=0, keepdims=True)
    small_send[0, 4:5, :chans] = jnp.sum(grad_conv * current[...].astype(jnp.float32), axis=0, keepdims=True)

    one_copy.wait_recv()
    mine = pl.ds(pl.multiple_of(part * rows, rows), rows)
    back_one = part_one[mine, :] + recv_one[...].astype(jnp.float32)
    own_tokens = tokens[mine, :].astype(jnp.float32)
    scale_one = norm_scale(own_tokens)
    grad_input[...] = (
        grad_resid[mine, :] + norm_back(own_tokens, scale_one, gain[0:1, :], back_one)
    ).astype(jnp.bfloat16)
    small_send[0, 0:1, :] = jnp.sum(back_one * own_tokens * scale_one, axis=0, keepdims=True)

    s_core = remote(small_send.at[0], small_core, s_send.at[0], s_recv.at[0], other_core)
    s_y = remote(small_send.at[1], small_y, s_send.at[1], s_recv.at[1], y_partner)
    s_z = [
        remote(small_send.at[2], small_z.at[k - 1], s_send.at[1 + k], s_recv.at[1 + k], z_partners[k])
        for k in range(1, DEPTH)
    ]
    s_x = remote(small_send.at[3], small_x, s_send.at[5], s_recv.at[5], x_partner)
    s_core.start()
    turn(7)
    s_core.wait_recv()
    small_send[1] = small_send[0] + small_core[...]
    s_y.start()
    turn(8)
    s_y.wait_recv()
    small_send[2] = small_send[1] + small_y[...]
    for copy in s_z:
        copy.start()
    turn(9)
    for copy in s_z:
        copy.wait_recv()
    small_send[3] = small_send[2] + small_z[0] + small_z[1] + small_z[2]
    s_x.start()
    turn(10)
    s_x.wait_recv()
    first = lax.broadcasted_iota(jnp.int32, small.shape, 0) == 0
    small[...] = small_send[3] + jnp.where(first, small_x[...], 0.0)
    for piece in range(11, count + 4):
        turn(piece)
    for copy in [two_copy, one_copy, head_copy, s_core, s_y, *s_z, s_x]:
        copy.wait_send()
    for piece in range(count):
        core_copy(piece).wait_send()
        y_copy(piece).wait_send()
        for k in range(1, DEPTH):
            z_copy(piece, k).wait_send()

def mixer_back(term_gu, term_down, values, seq):
    tall = seq // (DEPTH * CORES)
    group, width = values[1].shape
    chans = values[6].shape[1]
    depth = width // seq
    bf, fl = jnp.bfloat16, jnp.float32
    widths = [term_gu.shape[1], term_down.shape[1], chans, 3 * chans]
    pieces = pieces_of(widths, 768)
    ready = sum(1 for piece in pieces if piece[0] < 2)
    count = len(pieces)
    lead = (DEPTH, tall)
    dma = pltpu.SemaphoreType.DMA
    vmem = pltpu.VMEM
    in_vmem = pl.BlockSpec(memory_space=pltpu.VMEM)
    small = (8, width)
    big = [t.reshape((DEPTH, tall, CORES, depth, t.shape[1])) for t in (term_gu, term_down)]
    return pl.pallas_call(
        functools.partial(mixer_back_kernel, pieces, ready),
        out_shape=[jax.ShapeDtypeStruct((depth, w), fl) for w in widths]
        + [jax.ShapeDtypeStruct((group // 2, width), bf), jax.ShapeDtypeStruct(small, fl)],
        in_specs=[pl.BlockSpec(memory_space=pl.ANY)] * 2 + [in_vmem] * len(values),
        out_specs=[in_vmem] * 6,
        scratch_shapes=[vmem(lead + (depth, w), bf) for w in widths[:2]]
        + [vmem(lead + (CORES, depth, w), bf) for w in widths[2:]]
        + [vmem(lead + (depth, w), bf) for w in widths]
        + [vmem((DEPTH, depth, w), bf) for w in widths]
        + [vmem((DEPTH - 1, depth, w), bf) for w in widths]
        + [
            vmem((group, width), bf),
            vmem((group, width), fl),
            vmem((group, width), bf),
            vmem((group, 3 * chans), bf),
            vmem((group, width), fl),
            vmem((group // 2, width), bf),
            vmem((group // 2, width), bf),
            vmem((8, chans), fl),
            vmem((8, chans), fl),
            vmem((group, chans), fl),
            vmem((group, chans), fl),
            vmem((group, chans), fl),
            vmem((4,) + small, fl),
            vmem(small, fl),
            vmem(small, fl),
            vmem((DEPTH - 1,) + small, fl),
            vmem(small, fl),
            dma((count,)),
            dma((count,)),
            dma((count,)),
            dma((count,)),
            dma((count,)),
            dma((count, DEPTH)),
            dma((count, DEPTH)),
            dma((2,)),
            dma((2,)),
            dma((2,)),
            dma((6,)),
            dma((6,)),
        ],
        compiler_params=pltpu.CompilerParams(
            collective_id=2, has_side_effects=True, vmem_limit_bytes=60 * 1024 * 1024
        ),
        name="mixer_backward",
    )(*big, *values)


def mp_gather(value, axis):
    if lax.axis_size("mp") != 2:
        return lax.all_gather(value, "mp", axis=axis, tiled=True)
    other = lax.ppermute(value, "mp", [(0, 1), (1, 0)])
    first = lax.axis_index("mp") == 0
    return jnp.concatenate(
        [jnp.where(first, value, other), jnp.where(first, other, value)], axis=axis
    )


def mp_sum(value):
    if lax.axis_size("mp") != 2:
        return lax.psum(value, "mp")
    other = lax.ppermute(value.astype(jnp.bfloat16), "mp", [(0, 1), (1, 0)])
    return value + other.astype(jnp.float32)


def mp_sum_own(value, rows):
    if lax.axis_size("mp") != 2:
        return lax.psum_scatter(value, "mp", scatter_dimension=0, tiled=True)
    place = lax.axis_index("mp")
    sent = lax.dynamic_slice_in_dim(value, (1 - place) * rows, rows, 0).astype(jnp.bfloat16)
    other = lax.ppermute(sent, "mp", [(0, 1), (1, 0)])
    return lax.dynamic_slice_in_dim(value, place * rows, rows, 0) + other.astype(jnp.float32)


def on_device(tokens, positions, counts, cotangent, gains, in_w, out_w, gate_up, down_w, conv_w):
    rows, width = tokens.shape
    group = positions.shape[0]
    count = counts[0]
    seq = lax.axis_size("seq")
    wide = lax.axis_size("mp")
    mp_place = lax.axis_index("mp")
    depth = in_w.shape[0]
    chans = in_w.shape[2]
    units = gate_up.shape[2]
    gain_cols = width // seq
    tap_cols = chans // seq

    small = jnp.zeros((16, LANES), jnp.bfloat16)
    small = small.at[:2, :gain_cols].set(mp_gather(gains, 1))
    small = small.at[2:5, :tap_cols].set(conv_w)
    gathered, whole_rows = gather_all(
        [
            small,
            in_w.reshape(depth, 3 * chans),
            out_w.T,
            gate_up.reshape(depth, 2 * units),
            down_w.T,
        ],
        [tokens, cotangent],
        seq,
        wide,
    )
    small_all = gathered[0].reshape(seq, 16, LANES).astype(jnp.float32)
    in_flat = gathered[1].reshape(width, 3 * chans)
    out_turned = gathered[2].reshape(width, chans)
    gu_flat = gathered[3].reshape(width, 2 * units)
    down_turned = gathered[4].reshape(width, units)
    gain_all = small_all[:, :2, :gain_cols].transpose(1, 0, 2).reshape(2, width)
    conv_taps = small_all[:, 2:5, :tap_cols].transpose(1, 0, 2).reshape(3, chans)
    inputs = whole_rows[0].reshape(group, width).astype(jnp.float32)
    valid = (jnp.arange(group, dtype=jnp.int32) < count)[:, None]
    grad_all = whole_rows[1].reshape(group, width)
    grad_all = jnp.where(valid, grad_all, jnp.zeros_like(grad_all))

    def own(value):
        return lax.dynamic_slice_in_dim(value, mp_place * rows, rows, 0)

    scale_one = norm_scale(inputs)
    mixer_all = (inputs * scale_one * gain_all[0]).astype(jnp.bfloat16)
    proj = jnp.dot(mixer_all, in_flat, preferred_element_type=jnp.float32)
    bgate = proj[:, :chans]
    cgate = proj[:, chans : 2 * chans]
    xin = proj[:, 2 * chans :]
    gated = (bgate * xin).astype(jnp.bfloat16)
    tail = lax.dynamic_slice_in_dim(gated, count - 2, 2, 0)
    before = from_behind(tail, "seq", 1)
    extended = jnp.concatenate([before, gated], axis=0).astype(jnp.float32)
    one_back = extended[1 : group + 1]
    two_back = extended[:group]
    keep_one = (positions >= 1).astype(jnp.float32)[:, None]
    keep_two = (positions >= 2).astype(jnp.float32)[:, None]
    current = gated.astype(jnp.float32)
    conv = (
        conv_taps[2] * current
        + keep_one * conv_taps[1] * one_back
        + keep_two * conv_taps[0] * two_back
    )
    mixed_in = (cgate * conv).astype(jnp.bfloat16)
    resid = inputs + mp_sum(contract_cols(mixed_in, out_turned))
    scale_two = norm_scale(resid)
    ff_all = (resid * scale_two * gain_all[1]).astype(jnp.bfloat16)
    both = jnp.dot(ff_all, gu_flat, preferred_element_type=jnp.float32)
    gate = both[:, :units]
    upper = both[:, units:]
    sigma = jax.nn.sigmoid(gate)
    active = gate * sigma
    hidden = (active * upper).astype(jnp.bfloat16)
    final = own(resid) + mp_sum_own(contract_cols(hidden, down_turned), rows)
    mixed = jnp.where(own(valid), final, jnp.zeros_like(final)).astype(jnp.bfloat16)

    grad_hidden = jnp.dot(grad_all, down_turned, preferred_element_type=jnp.float32)
    slope = sigma * (1.0 + gate * (1.0 - sigma))
    grad_both = jnp.concatenate([grad_hidden * upper * slope, grad_hidden * active], axis=1).astype(
        jnp.bfloat16
    )
    term_down = contract_rows(grad_all, hidden).astype(jnp.bfloat16)
    term_gu = contract_rows(ff_all, grad_both).astype(jnp.bfloat16)
    partial_two = contract_cols(grad_both, gu_flat)
    if wide == 2 and seq == DEPTH * 2 * CORES:
        row_ids = jnp.arange(group, dtype=jnp.int32)[:, None]
        masks = jnp.concatenate(
            [
                keep_one,
                keep_two,
                (row_ids == count - 2).astype(jnp.float32),
                (row_ids == count - 1).astype(jnp.float32),
            ],
            axis=1,
        )
        sum_gu, sum_down, sum_out, sum_in, grad_input, small_sums = mixer_back(
            term_gu,
            term_down,
            [
                partial_two.astype(jnp.bfloat16),
                partial_two,
                resid,
                grad_all,
                whole_rows[0].reshape(group, width),
                mixer_all,
                mixed_in,
                conv,
                cgate,
                xin,
                bgate,
                gated,
                one_back,
                two_back,
                masks,
                out_turned,
                in_flat,
                gain_all,
                conv_taps,
            ],
            seq,
        )
        here = lax.axis_index("seq")
        gain_size = gains.shape[1]
        return (
            mixed,
            grad_input,
            lax.dynamic_slice(small_sums, (0, (here * wide + mp_place) * gain_size), (2, gain_size)),
            sum_in.reshape(depth, 3, chans),
            sum_out.T,
            sum_gu.reshape(depth, 2, units),
            sum_down.T,
            lax.dynamic_slice(small_sums, (2, here * tap_cols), (3, tap_cols)),
        )
    back_two = mp_sum(partial_two)
    grad_resid = grad_all.astype(jnp.float32) + norm_back(resid, scale_two, gain_all[1], back_two)
    gain_two = jnp.sum(own(back_two * resid * scale_two), axis=0)
    grad_o_all = grad_resid.astype(jnp.bfloat16)
    term_out = contract_rows(grad_o_all, mixed_in).astype(jnp.bfloat16)
    grad_mix = jnp.dot(grad_o_all, out_turned, preferred_element_type=jnp.float32)
    grad_cgate = grad_mix * conv
    grad_conv = grad_mix * cgate
    lead_one = keep_one * grad_conv
    lead_two = keep_two * grad_conv
    head = jnp.stack(
        [conv_taps[0] * lead_two[0], conv_taps[1] * lead_one[0] + conv_taps[0] * lead_two[1]]
    )
    after = from_behind(head, "seq", -1)
    zero_one = jnp.zeros((1, chans), jnp.float32)
    zero_two = jnp.zeros((2, chans), jnp.float32)
    row_ids = jnp.arange(group, dtype=jnp.int32)[:, None]
    border = jnp.where(row_ids == count - 2, after[:1], jnp.where(row_ids == count - 1, after[1:], 0.0))
    grad_gated = (
        conv_taps[2] * grad_conv
        + conv_taps[1] * jnp.concatenate([lead_one[1:], zero_one], axis=0)
        + conv_taps[0] * jnp.concatenate([lead_two[2:], zero_two], axis=0)
        + border
    )
    term_conv = jnp.stack(
        [
            jnp.sum(lead_two * two_back, axis=0),
            jnp.sum(lead_one * one_back, axis=0),
            jnp.sum(grad_conv * current, axis=0),
        ]
    )
    grad_proj = jnp.concatenate([grad_gated * xin, grad_cgate, grad_gated * bgate], axis=1).astype(
        jnp.bfloat16
    )
    term_in = contract_rows(mixer_all, grad_proj).astype(jnp.bfloat16)
    back_one = mp_sum_own(contract_cols(grad_proj, in_flat), rows)
    own_inputs = own(inputs)
    own_scale = own(scale_one)
    grad_input = (
        own(grad_resid) + norm_back(own_inputs, own_scale, gain_all[0], back_one)
    ).astype(jnp.bfloat16)
    gain_one = jnp.sum(back_one * own_inputs * own_scale, axis=0)
    gain_terms = jnp.stack([gain_one, gain_two]).reshape(2, seq, gain_cols).transpose(1, 0, 2)
    tap_terms = term_conv.reshape(3, seq, tap_cols).transpose(1, 0, 2)
    small_terms = jnp.zeros((seq, 8, LANES), jnp.float32)
    small_terms = small_terms.at[:, :2, :gain_cols].set(gain_terms)
    small_terms = small_terms.at[:, 2:5, :tap_cols].set(tap_terms)
    sum_gu, sum_down, sum_out, sum_in, sum_small = scatter_all(
        [term_gu, term_down, term_out, term_in, small_terms.reshape(seq * 8, LANES)], seq
    )
    grad_gains = lax.psum_scatter(
        sum_small[:2, :gain_cols], "mp", scatter_dimension=1, tiled=True
    ) if wide != 2 else gain_share(sum_small[:2, :gain_cols], mp_place)
    return (
        mixed,
        grad_input,
        grad_gains,
        sum_in.reshape(depth, 3, chans),
        sum_out.T,
        sum_gu.reshape(depth, 2, units),
        sum_down.T,
        sum_small[2:5, :tap_cols],
    )


def gain_share(sums, place):
    cols = sums.shape[1] // 2
    total = sums + lax.ppermute(sums, "mp", [(0, 1), (1, 0)])
    return lax.dynamic_slice_in_dim(total, place * cols, cols, 1)


def solution(mesh):
    placed = (
        P(("seq", "mp"), None),
        P("seq"),
        P("seq"),
        P(("seq", "mp"), None),
        P(None, ("seq", "mp")),
        P("seq", None, "mp"),
        P("mp", "seq"),
        P("seq", None, "mp"),
        P("mp", "seq"),
        P(None, ("mp", "seq")),
    )
    return jax.shard_map(
        on_device,
        mesh=mesh,
        in_specs=placed,
        out_specs=(
            P(("seq", "mp"), None),
            P(("seq", "mp"), None),
            P(None, ("seq", "mp")),
            P("seq", None, "mp"),
            P("mp", "seq"),
            P("seq", None, "mp"),
            P("mp", "seq"),
            P(None, ("mp", "seq")),
        ),
        check_vma=False,
    )
```

```python
import functools

import jax
import jax.numpy as jnp
from jax import lax
from jax.experimental import pallas as pl
from jax.experimental.pallas import tpu as pltpu
from jax.sharding import PartitionSpec as P

eps = 1e-05
MESH = pl.DeviceIdType.MESH
DEPTH = 4
CORES = 2
LANES = 128
VMEM_BYTES = 58 * 1024 * 1024


def contract_rows(left, right):
    return lax.dot_general(
        left, right, (((0,), (0,)), ((), ())), preferred_element_type=jnp.float32
    )


def contract_cols(left, right):
    return lax.dot_general(
        left, right, (((1,), (1,)), ((), ())), preferred_element_type=jnp.float32
    )


def norm_scale(values):
    return lax.rsqrt(jnp.mean(values * values, axis=-1, keepdims=True) + eps)


def norm_back(values, scale, gain, grad):
    weighted = grad * gain
    cubed = scale * scale * scale
    return scale * weighted - values * cubed * jnp.mean(weighted * values, axis=-1, keepdims=True)


def from_behind(value, axis, steps):
    count = lax.axis_size(axis)
    leading, last = (max(0, -steps), min(count, count - steps))
    return lax.ppermute(value, axis, [(source, source + steps) for source in range(leading, last)])


def pieces_of(widths, size, fine=None):
    pieces = []
    for place, width in enumerate(widths):
        step = size // 2 if place == fine else size
        step = step if width % step == 0 else width
        pieces.extend((place, start, step) for start in range(0, width, step))
    return pieces


def seq_place(tall):
    here = lax.axis_index("seq")
    core = lax.rem(here, CORES)
    chip = here // CORES
    return chip // tall, lax.rem(chip, tall), core


def seq_index(tall, z, y, core):
    return (z * tall + y) * CORES + core


def greet(partners):
    barrier = pltpu.get_barrier_semaphore()
    for partner in partners:
        pl.semaphore_signal(barrier, inc=1, device_id=partner, device_id_type=MESH)
    pl.semaphore_wait(barrier, len(partners))


def remote(source, target, send, recv, partner):
    return pltpu.make_async_remote_copy(
        src_ref=source,
        dst_ref=target,
        send_sem=send,
        recv_sem=recv,
        device_id=partner,
        device_id_type=MESH,
    )


def gather_kernel(pieces, arrays, halves, tall, wide, *refs):
    ins = refs[:arrays]
    rows_in = refs[arrays : arrays + halves]
    outs = refs[arrays + halves : 2 * arrays + halves]
    rows_out = refs[2 * arrays + halves : 2 * (arrays + halves)]
    (own_sem, z_send, z_recv, y_send, y_recv, c_send, c_recv, x_send, x_recv) = refs[
        2 * (arrays + halves) :
    ]
    z, y, core = seq_place(tall)
    part = lax.axis_index("mp")

    def at_z(step):
        return lax.rem(z + step + DEPTH, DEPTH)

    def at_y(step):
        return lax.rem(y + step + tall, tall)

    other_core = {"seq": seq_index(tall, z, y, 1 - core)}
    z_partners = {k: {"seq": seq_index(tall, at_z(k), y, core)} for k in range(1, DEPTH)}
    y_partners = {j: {"seq": seq_index(tall, z, at_y(j), core)} for j in range(1, tall)}
    x_partners = {i: {"mp": lax.rem(part + i, wide)} for i in range(1, wide)}
    greet(
        [other_core, *z_partners.values(), *y_partners.values(), *x_partners.values()]
    )

    def slot(piece, zz, yy, cc):
        place, start, width = pieces[piece]
        return outs[place].at[zz, yy, cc, :, pl.ds(start, width)]

    def own(piece):
        place, start, width = pieces[piece]
        return ins[place].at[:, pl.ds(start, width)]

    waits = []

    def begin(copy):
        copy.start()
        waits.append(copy)

    def send_y(piece, k):
        source = own(piece) if k == 0 else slot(piece, at_z(-k), y, core)
        for j in range(1, tall):
            begin(
                remote(
                    source,
                    slot(piece, at_z(-k), y, core),
                    y_send.at[piece, k, j],
                    y_recv.at[piece, k, j],
                    y_partners[j],
                )
            )

    def send_core(piece, k, j):
        target = slot(piece, at_z(-k), at_y(-j), core)
        source = own(piece) if k == 0 and j == 0 else target
        begin(
            remote(
                source, target, c_send.at[piece, k, j], c_recv.at[piece, k, j], other_core
            )
        )

    def send_z(piece):
        for k in range(1, DEPTH):
            begin(
                remote(
                    own(piece),
                    slot(piece, z, y, core),
                    z_send.at[piece, k],
                    z_recv.at[piece, k],
                    z_partners[k],
                )
            )

    ahead = 3
    for piece in range(min(ahead, len(pieces))):
        send_z(piece)
    for piece in range(len(pieces)):
        send_y(piece, 0)
        if piece == 0:
            for index in range(halves):
                for i in range(1, wide):
                    begin(
                        remote(
                            rows_in[index],
                            rows_out[index].at[part],
                            x_send.at[index, i],
                            x_recv.at[index, i],
                            x_partners[i],
                        )
                    )
    locals_ = []
    for place in range(arrays):
        copy = pltpu.make_async_copy(
            ins[place], outs[place].at[z, y, core], own_sem.at[place]
        )
        copy.start()
        locals_.append(copy)
    for index in range(halves):
        copy = pltpu.make_async_copy(
            rows_in[index], rows_out[index].at[part], own_sem.at[arrays + index]
        )
        copy.start()
        locals_.append(copy)
    for piece in range(len(pieces)):
        send_core(piece, 0, 0)

    def from_z(piece):
        for k in range(1, DEPTH):
            landed = slot(piece, at_z(-k), y, core)
            remote(
                landed, landed, z_send.at[piece, k], z_recv.at[piece, k], z_partners[k]
            ).wait_recv()
            send_y(piece, k)
            send_core(piece, k, 0)
        if piece + ahead < len(pieces):
            send_z(piece + ahead)

    def from_y(piece):
        for k in range(DEPTH):
            for j in range(1, tall):
                landed = slot(piece, at_z(-k), at_y(-j), core)
                remote(
                    landed,
                    landed,
                    y_send.at[piece, k, j],
                    y_recv.at[piece, k, j],
                    y_partners[j],
                ).wait_recv()
                send_core(piece, k, j)

    for piece in range(len(pieces) + 1):
        if piece < len(pieces):
            from_z(piece)
        if piece > 0:
            from_y(piece - 1)
    for piece in range(len(pieces)):
        for k in range(DEPTH):
            for j in range(tall):
                landed = slot(piece, at_z(-k), at_y(-j), 1 - core)
                remote(
                    landed,
                    landed,
                    c_send.at[piece, k, j],
                    c_recv.at[piece, k, j],
                    other_core,
                ).wait_recv()
    for index in range(halves):
        for i in range(1, wide):
            landed = rows_out[index].at[lax.rem(part - i + wide, wide)]
            remote(
                landed, landed, x_send.at[index, i], x_recv.at[index, i], x_partners[i]
            ).wait_recv()
    for copy in waits:
        copy.wait_send()
    for copy in locals_:
        copy.wait()


def gather_all(shards, row_parts, seq, wide):
    tall = seq // (DEPTH * CORES)
    pieces = pieces_of([shard.shape[1] for shard in shards], 768, len(shards) - 1)
    count = len(pieces)
    moved = sum(shard.size * shard.dtype.itemsize for shard in shards) * seq
    dma = pltpu.SemaphoreType.DMA
    halves = len(row_parts)
    results = pl.pallas_call(
        functools.partial(gather_kernel, pieces, len(shards), halves, tall, wide),
        out_shape=[
            jax.ShapeDtypeStruct((DEPTH, tall, CORES) + shard.shape, shard.dtype)
            for shard in shards
        ]
        + [jax.ShapeDtypeStruct((wide,) + part.shape, part.dtype) for part in row_parts],
        in_specs=[pl.BlockSpec(memory_space=pl.ANY)] * (len(shards) + halves),
        out_specs=[pl.BlockSpec(memory_space=pl.ANY)] * (len(shards) + halves),
        scratch_shapes=[
            dma((len(shards) + halves,)),
            dma((count, DEPTH)),
            dma((count, DEPTH)),
            dma((count, DEPTH, tall)),
            dma((count, DEPTH, tall)),
            dma((count, DEPTH, tall)),
            dma((count, DEPTH, tall)),
            dma((halves, wide)),
            dma((halves, wide)),
        ],
        compiler_params=pltpu.CompilerParams(collective_id=0, has_side_effects=True),
        cost_estimate=pl.CostEstimate(flops=0, bytes_accessed=16 * moved, transcendentals=0),
        name="gather_weights",
    )(*shards, *row_parts)
    return results[: len(shards)], results[len(shards) :]


def scatter_kernel(pieces, arrays, tall, *refs):
    ins = refs[:arrays]
    outs = refs[arrays : 2 * arrays]
    rest = refs[2 * arrays :]
    from_core = rest[:arrays]
    from_y = rest[arrays : 2 * arrays]
    summed = rest[2 * arrays : 3 * arrays]
    from_z = rest[3 * arrays : 4 * arrays]
    c_send, c_recv, y_send, y_recv, z_send, z_recv = rest[4 * arrays :]
    z, y, core = seq_place(tall)

    def at_z(step):
        return lax.rem(z + step + DEPTH, DEPTH)

    def at_y(step):
        return lax.rem(y + step + tall, tall)

    other_core = {"seq": seq_index(tall, z, y, 1 - core)}
    z_partners = {k: {"seq": seq_index(tall, at_z(k), y, core)} for k in range(1, DEPTH)}
    y_partners = {j: {"seq": seq_index(tall, z, at_y(j), core)} for j in range(1, tall)}
    greet([other_core, *z_partners.values(), *y_partners.values()])

    def core_copy(piece):
        place, start, width = pieces[piece]
        cols = pl.ds(start, width)
        return remote(
            ins[place].at[:, :, 1 - core, :, cols],
            from_core[place].at[:, :, :, cols],
            c_send.at[piece],
            c_recv.at[piece],
            other_core,
        )

    def y_copy(piece, j):
        place, start, width = pieces[piece]
        cols = pl.ds(start, width)
        return remote(
            from_core[place].at[:, at_y(j), :, cols],
            from_y[place].at[j - 1, :, :, cols],
            y_send.at[piece, j],
            y_recv.at[piece, j],
            y_partners[j],
        )

    def z_copy(piece, k):
        place, start, width = pieces[piece]
        cols = pl.ds(start, width)
        return remote(
            summed[place].at[at_z(k), :, cols],
            from_z[place].at[k - 1, :, cols],
            z_send.at[piece, k],
            z_recv.at[piece, k],
            z_partners[k],
        )

    def after_core(piece):
        place, start, width = pieces[piece]
        cols = pl.ds(start, width)
        core_copy(piece).wait_recv()

        def add(block, carry):
            zz = block // tall
            yy = lax.rem(block, tall)
            total = ins[place][zz, yy, core, :, cols].astype(jnp.float32) + from_core[place][
                zz, yy, :, cols
            ].astype(jnp.float32)
            from_core[place][zz, yy, :, cols] = total.astype(from_core[place].dtype)
            return carry

        lax.fori_loop(0, DEPTH * tall, add, 0)
        for j in range(1, tall):
            y_copy(piece, j).start()

    def after_y(piece):
        place, start, width = pieces[piece]
        cols = pl.ds(start, width)
        for j in range(1, tall):
            y_copy(piece, j).wait_recv()

        def add(zz, carry):
            total = from_core[place][zz, y, :, cols].astype(jnp.float32)
            for j in range(1, tall):
                total = total + from_y[place][j - 1, zz, :, cols].astype(jnp.float32)
            summed[place][zz, :, cols] = total.astype(summed[place].dtype)
            return carry

        lax.fori_loop(0, DEPTH, add, 0)
        for k in range(1, DEPTH):
            z_copy(piece, k).start()

    def after_z(piece):
        place, start, width = pieces[piece]
        cols = pl.ds(start, width)
        for k in range(1, DEPTH):
            z_copy(piece, k).wait_recv()
        total = summed[place][z, :, cols].astype(jnp.float32)
        for k in range(1, DEPTH):
            total = total + from_z[place][k - 1, :, cols].astype(jnp.float32)
        outs[place][:, cols] = total

    count = len(pieces)
    for piece in range(count):
        core_copy(piece).start()
    for piece in range(count + 4):
        if piece < count:
            after_core(piece)
        if 2 <= piece < count + 2:
            after_y(piece - 2)
        if 4 <= piece:
            after_z(piece - 4)
    for piece in range(count):
        core_copy(piece).wait_send()
        for j in range(1, tall):
            y_copy(piece, j).wait_send()
        for k in range(1, DEPTH):
            z_copy(piece, k).wait_send()


def scatter_all(terms, seq):
    tall = seq // (DEPTH * CORES)
    terms = [
        term.reshape((DEPTH, tall, CORES, term.shape[0] // seq, term.shape[1])) for term in terms
    ]
    blocks = [term.shape[3:] for term in terms]
    kinds = [term.dtype for term in terms]
    pieces = pieces_of([block[1] for block in blocks], 768)
    count = len(pieces)
    pairs = list(zip(blocks, kinds))
    dma = pltpu.SemaphoreType.DMA
    return pl.pallas_call(
        functools.partial(scatter_kernel, pieces, len(terms), tall),
        out_shape=[jax.ShapeDtypeStruct(block, jnp.float32) for block in blocks],
        in_specs=[pl.BlockSpec(memory_space=pltpu.VMEM)] * len(terms),
        out_specs=[pl.BlockSpec(memory_space=pltpu.VMEM)] * len(terms),
        scratch_shapes=[pltpu.VMEM((DEPTH, tall) + block, kind) for block, kind in pairs]
        + [pltpu.VMEM((max(1, tall - 1), DEPTH) + block, kind) for block, kind in pairs]
        + [pltpu.VMEM((DEPTH,) + block, kind) for block, kind in pairs]
        + [pltpu.VMEM((DEPTH - 1,) + block, kind) for block, kind in pairs]
        + [
            dma((count,)),
            dma((count,)),
            dma((count, tall)),
            dma((count, tall)),
            dma((count, DEPTH)),
            dma((count, DEPTH)),
        ],
        compiler_params=pltpu.CompilerParams(
            collective_id=1, has_side_effects=True, vmem_limit_bytes=VMEM_BYTES
        ),
        name="scatter_grads",
    )(*terms)


def mixer_back_kernel(pieces, ready, *refs):
    (gu_hbm, down_hbm, sent_two, part_two, resid, grad_all, tokens, mixer, mixed_in, conv, cgate, xin,
     bgate, current, one_back, two_back, masks, out_w, in_w, gain, taps) = refs[:21]
    sum_gu, sum_down, sum_out, sum_in, grad_input, small = refs[21:27]
    rest = refs[27:]
    own_gu, own_down, term_out, term_in = rest[:4]
    from_core = rest[4:8]
    from_y = rest[8:12]
    from_z = rest[12:16]
    (recv_two, grad_resid, grad_o, grad_proj, part_one, send_one, recv_one, head, after, lead_one_ref,
     lead_two_ref, gconv_ref, small_send, small_core, small_y, small_z, small_x) = rest[16:33]
    (l_sem, c_send, c_recv, y_send, y_recv, z_send, z_recv, x_send, x_recv, h_sem, s_send, s_recv) = rest[33:]
    outs = (sum_gu, sum_down, sum_out, sum_in)
    terms = (gu_hbm, down_hbm, term_out, term_in)
    tall = 2
    total_seq = DEPTH * tall * CORES
    group = resid.shape[0]
    rows = grad_input.shape[0]
    chans = conv.shape[1]
    z, y, core = seq_place(tall)
    here = lax.axis_index("seq")
    part = lax.axis_index("mp")

    def at_z(step):
        return lax.rem(z + step + DEPTH, DEPTH)

    other_core = {"seq": seq_index(tall, z, y, 1 - core)}
    z_partners = {k: {"seq": seq_index(tall, at_z(k), y, core)} for k in range(1, DEPTH)}
    y_partner = {"seq": seq_index(tall, z, 1 - y, core)}
    x_partner = {"mp": 1 - part}
    earlier = {"seq": lax.rem(here + total_seq - 1, total_seq)}
    later = {"seq": lax.rem(here + 1, total_seq)}
    greet([other_core, *z_partners.values(), y_partner, x_partner, earlier, later])

    def core_copy(piece):
        place, start, width = pieces[piece]
        cols = pl.ds(start, width)
        return remote(terms[place].at[:, :, 1 - core, :, cols], from_core[place].at[:, :, :, cols],
                      c_send.at[piece], c_recv.at[piece], other_core)

    def own_copy(piece):
        place, start, width = pieces[piece]
        cols = pl.ds(start, width)
        return pltpu.make_async_copy(terms[place].at[:, :, core, :, cols],
                                     (own_gu, own_down)[place].at[:, :, :, cols], l_sem.at[piece])

    def y_copy(piece):
        place, start, width = pieces[piece]
        cols = pl.ds(start, width)
        return remote(from_core[place].at[:, 1 - y, :, cols], from_y[place].at[:, :, cols],
                      y_send.at[piece], y_recv.at[piece], y_partner)

    def z_copy(piece, k):
        place, start, width = pieces[piece]
        cols = pl.ds(start, width)
        return remote(from_y[place].at[at_z(k), :, cols], from_z[place].at[k - 1, :, cols],
                      z_send.at[piece, k], z_recv.at[piece, k], z_partners[k])

    def after_core(piece):
        place, start, width = pieces[piece]
        cols = pl.ds(start, width)
        if piece < ready:
            own_copy(piece).wait()
        core_copy(piece).wait_recv()

        def add(block, carry):
            zz = block // tall
            yy = lax.rem(block, tall)
            if place < 2:
                mine = (own_gu, own_down)[place][zz, yy, :, cols]
            else:
                mine = terms[place][zz, yy, core, :, cols]
            total = mine.astype(jnp.float32) + from_core[place][zz, yy, :, cols].astype(jnp.float32)
            from_core[place][zz, yy, :, cols] = total.astype(jnp.bfloat16)
            return carry

        lax.fori_loop(0, DEPTH * tall, add, 0)
        y_copy(piece).start()

    def after_y(piece):
        place, start, width = pieces[piece]
        cols = pl.ds(start, width)
        y_copy(piece).wait_recv()

        def add(zz, carry):
            total = from_core[place][zz, y, :, cols].astype(jnp.float32) + from_y[place][
                zz, :, cols
            ].astype(jnp.float32)
            from_y[place][zz, :, cols] = total.astype(jnp.bfloat16)
            return carry

        lax.fori_loop(0, DEPTH, add, 0)
        for k in range(1, DEPTH):
            z_copy(piece, k).start()

    def after_z(piece):
        place, start, width = pieces[piece]
        cols = pl.ds(start, width)
        for k in range(1, DEPTH):
            z_copy(piece, k).wait_recv()
        total = from_y[place][z, :, cols].astype(jnp.float32)
        for k in range(1, DEPTH):
            total = total + from_z[place][k - 1, :, cols].astype(jnp.float32)
        outs[place][:, cols] = total

    two_copy = remote(sent_two, recv_two, x_send.at[0], x_recv.at[0], x_partner)
    one_copy = remote(send_one, recv_one, x_send.at[1], x_recv.at[1], x_partner)
    head_copy = remote(head, after, h_sem.at[0], h_sem.at[1], earlier)

    count = len(pieces)
    ahead = 3

    def begin_core(piece):
        core_copy(piece).start()
        if piece < ready:
            own_copy(piece).start()

    def turn(piece):
        if piece < count:
            after_core(piece)
            if piece + ahead < ready:
                begin_core(piece + ahead)
        if 0 <= piece - 2 < count:
            after_y(piece - 2)
        if 0 <= piece - 4 < count:
            after_z(piece - 4)

    two_copy.start()
    for piece in range(ahead):
        begin_core(piece)
    turn(0)
    turn(1)

    two_copy.wait_recv()
    gain_two_row = gain[1:2, :]
    step = 32

    def residual(block, acc):
        at = pl.ds(pl.multiple_of(block * step, step), step)
        back = part_two[at, :] + recv_two[at, :].astype(jnp.float32)
        value = resid[at, :]
        scale = norm_scale(value)
        grad = grad_all[at, :].astype(jnp.float32) + norm_back(value, scale, gain_two_row, back)
        grad_resid[at, :] = grad
        grad_o[at, :] = grad.astype(jnp.bfloat16)
        return acc + jnp.sum(back * value * scale, axis=0, keepdims=True)

    gain_two = lax.fori_loop(0, group // step, residual, jnp.zeros((1, resid.shape[1]), jnp.float32))
    small_send[0] = jnp.zeros(small_send.shape[1:], jnp.float32)
    small_send[0, 1:2, :] = gain_two

    turn(2)

    keep_one = masks[:, 0:1]
    keep_two = masks[:, 1:2]
    grad_mix = jnp.dot(grad_o[...], out_w[...], preferred_element_type=jnp.float32)
    grad_proj[:, chans : 2 * chans] = (grad_mix * conv[...]).astype(jnp.bfloat16)
    grad_conv = grad_mix * cgate[...]
    lead_one = keep_one * grad_conv
    lead_two = keep_two * grad_conv
    head[...] = jnp.zeros_like(head)
    head[0:1, :] = taps[0:1, :] * lead_two[0:1, :]
    head[1:2, :] = taps[1:2, :] * lead_one[0:1, :] + taps[0:1, :] * lead_two[1:2, :]
    head_copy.start()
    lead_one_ref[...] = lead_one
    lead_two_ref[...] = lead_two
    gconv_ref[...] = grad_conv
    turn(3)
    block = group

    def out_block(zz, carry):
        at = pl.ds(pl.multiple_of(zz * block, block), block)
        value = contract_rows(grad_o[:, at], mixed_in[...])
        term_out[zz] = value.astype(jnp.bfloat16).reshape(term_out.shape[1:])
        return carry

    lax.fori_loop(0, DEPTH, out_block, 0)
    turn(4)
    begin_core(ready)

    head_copy.wait_recv()
    lead_one = lead_one_ref[...]
    lead_two = lead_two_ref[...]
    grad_conv = gconv_ref[...]
    row_ids = lax.broadcasted_iota(jnp.int32, (group, chans), 0)
    moved_one = jnp.where(row_ids < group - 1, pltpu.roll(lead_one, group - 1, 0), 0.0)
    moved_two = jnp.where(row_ids < group - 2, pltpu.roll(lead_two, group - 2, 0), 0.0)
    border = masks[:, 2:3] * after[0:1, :] + masks[:, 3:4] * after[1:2, :]
    border = jnp.where(here == total_seq - 1, jnp.zeros_like(border), border)
    grad_gated = taps[2:3, :] * grad_conv + taps[1:2, :] * moved_one + taps[0:1, :] * moved_two + border
    grad_proj[:, :chans] = (grad_gated * xin[...]).astype(jnp.bfloat16)
    grad_proj[:, 2 * chans :] = (grad_gated * bgate[...]).astype(jnp.bfloat16)
    part_one[...] = contract_cols(grad_proj[...], in_w[...])
    send_one[...] = part_one[pl.ds(pl.multiple_of((1 - part) * rows, rows), rows), :].astype(jnp.bfloat16)
    one_copy.start()

    turn(5)

    def in_block(zz, carry):
        at = pl.ds(pl.multiple_of(zz * block, block), block)
        value = contract_rows(mixer[:, at], grad_proj[...])
        term_in[zz] = value.astype(jnp.bfloat16).reshape(term_in.shape[1:])
        return carry

    lax.fori_loop(0, DEPTH, in_block, 0)
    for piece in range(ready + 1, count):
        begin_core(piece)
    turn(6)
    small_send[0, 2:3, :chans] = jnp.sum(lead_two * two_back[...], axis=0, keepdims=True)
    small_send[0, 3:4, :chans] = jnp.sum(lead_one * one_back[...], axis=0, keepdims=True)
    small_send[0, 4:5, :chans] = jnp.sum(grad_conv * current[...].astype(jnp.float32), axis=0, keepdims=True)

    one_copy.wait_recv()
    mine = pl.ds(pl.multiple_of(part * rows, rows), rows)
    back_one = part_one[mine, :] + recv_one[...].astype(jnp.float32)
    own_tokens = tokens[mine, :].astype(jnp.float32)
    scale_one = norm_scale(own_tokens)
    grad_input[...] = (
        grad_resid[mine, :] + norm_back(own_tokens, scale_one, gain[0:1, :], back_one)
    ).astype(jnp.bfloat16)
    small_send[0, 0:1, :] = jnp.sum(back_one * own_tokens * scale_one, axis=0, keepdims=True)

    s_core = remote(small_send.at[0], small_core, s_send.at[0], s_recv.at[0], other_core)
    s_y = remote(small_send.at[1], small_y, s_send.at[1], s_recv.at[1], y_partner)
    s_z = [
        remote(small_send.at[2], small_z.at[k - 1], s_send.at[1 + k], s_recv.at[1 + k], z_partners[k])
        for k in range(1, DEPTH)
    ]
    s_x = remote(small_send.at[3], small_x, s_send.at[5], s_recv.at[5], x_partner)
    s_core.start()
    turn(7)
    s_core.wait_recv()
    small_send[1] = small_send[0] + small_core[...]
    s_y.start()
    turn(8)
    s_y.wait_recv()
    small_send[2] = small_send[1] + small_y[...]
    for copy in s_z:
        copy.start()
    turn(9)
    for copy in s_z:
        copy.wait_recv()
    small_send[3] = small_send[2] + small_z[0] + small_z[1] + small_z[2]
    s_x.start()
    turn(10)
    s_x.wait_recv()
    first = lax.broadcasted_iota(jnp.int32, small.shape, 0) == 0
    small[...] = small_send[3] + jnp.where(first, small_x[...], 0.0)
    for piece in range(11, count + 4):
        turn(piece)
    for copy in [two_copy, one_copy, head_copy, s_core, s_y, *s_z, s_x]:
        copy.wait_send()
    for piece in range(count):
        core_copy(piece).wait_send()
        y_copy(piece).wait_send()
        for k in range(1, DEPTH):
            z_copy(piece, k).wait_send()

def mixer_back(term_gu, term_down, values, seq):
    tall = seq // (DEPTH * CORES)
    group, width = values[1].shape
    chans = values[6].shape[1]
    depth = width // seq
    bf, fl = jnp.bfloat16, jnp.float32
    widths = [term_gu.shape[1], term_down.shape[1], chans, 3 * chans]
    pieces = pieces_of(widths, 768, len(widths) - 1)
    ready = sum(1 for piece in pieces if piece[0] < 2)
    count = len(pieces)
    lead = (DEPTH, tall)
    dma = pltpu.SemaphoreType.DMA
    vmem = pltpu.VMEM
    in_vmem = pl.BlockSpec(memory_space=pltpu.VMEM)
    small = (8, width)
    big = [t.reshape((DEPTH, tall, CORES, depth, t.shape[1])) for t in (term_gu, term_down)]
    return pl.pallas_call(
        functools.partial(mixer_back_kernel, pieces, ready),
        out_shape=[jax.ShapeDtypeStruct((depth, w), fl) for w in widths]
        + [jax.ShapeDtypeStruct((group // 2, width), bf), jax.ShapeDtypeStruct(small, fl)],
        in_specs=[pl.BlockSpec(memory_space=pl.ANY)] * 2 + [in_vmem] * len(values),
        out_specs=[in_vmem] * 6,
        scratch_shapes=[vmem(lead + (depth, w), bf) for w in widths[:2]]
        + [vmem(lead + (CORES, depth, w), bf) for w in widths[2:]]
        + [vmem(lead + (depth, w), bf) for w in widths]
        + [vmem((DEPTH, depth, w), bf) for w in widths]
        + [vmem((DEPTH - 1, depth, w), bf) for w in widths]
        + [
            vmem((group, width), bf),
            vmem((group, width), fl),
            vmem((group, width), bf),
            vmem((group, 3 * chans), bf),
            vmem((group, width), fl),
            vmem((group // 2, width), bf),
            vmem((group // 2, width), bf),
            vmem((8, chans), fl),
            vmem((8, chans), fl),
            vmem((group, chans), fl),
            vmem((group, chans), fl),
            vmem((group, chans), fl),
            vmem((4,) + small, fl),
            vmem(small, fl),
            vmem(small, fl),
            vmem((DEPTH - 1,) + small, fl),
            vmem(small, fl),
            dma((count,)),
            dma((count,)),
            dma((count,)),
            dma((count,)),
            dma((count,)),
            dma((count, DEPTH)),
            dma((count, DEPTH)),
            dma((2,)),
            dma((2,)),
            dma((2,)),
            dma((6,)),
            dma((6,)),
        ],
        compiler_params=pltpu.CompilerParams(
            collective_id=2, has_side_effects=True, vmem_limit_bytes=60 * 1024 * 1024
        ),
        name="mixer_backward",
    )(*big, *values)


def mp_gather(value, axis):
    if lax.axis_size("mp") != 2:
        return lax.all_gather(value, "mp", axis=axis, tiled=True)
    other = lax.ppermute(value, "mp", [(0, 1), (1, 0)])
    first = lax.axis_index("mp") == 0
    return jnp.concatenate(
        [jnp.where(first, value, other), jnp.where(first, other, value)], axis=axis
    )


def mp_sum(value):
    if lax.axis_size("mp") != 2:
        return lax.psum(value, "mp")
    other = lax.ppermute(value.astype(jnp.bfloat16), "mp", [(0, 1), (1, 0)])
    return value + other.astype(jnp.float32)


def mp_sum_own(value, rows):
    if lax.axis_size("mp") != 2:
        return lax.psum_scatter(value, "mp", scatter_dimension=0, tiled=True)
    place = lax.axis_index("mp")
    sent = lax.dynamic_slice_in_dim(value, (1 - place) * rows, rows, 0).astype(jnp.bfloat16)
    other = lax.ppermute(sent, "mp", [(0, 1), (1, 0)])
    return lax.dynamic_slice_in_dim(value, place * rows, rows, 0) + other.astype(jnp.float32)


def on_device(tokens, positions, counts, cotangent, gains, in_w, out_w, gate_up, down_w, conv_w):
    rows, width = tokens.shape
    group = positions.shape[0]
    count = counts[0]
    seq = lax.axis_size("seq")
    wide = lax.axis_size("mp")
    mp_place = lax.axis_index("mp")
    depth = in_w.shape[0]
    chans = in_w.shape[2]
    units = gate_up.shape[2]
    gain_cols = width // seq
    tap_cols = chans // seq

    small = jnp.zeros((16, LANES), jnp.bfloat16)
    small = small.at[:2, :gain_cols].set(mp_gather(gains, 1))
    small = small.at[2:5, :tap_cols].set(conv_w)
    gathered, whole_rows = gather_all(
        [
            small,
            in_w.reshape(depth, 3 * chans),
            out_w.T,
            gate_up.reshape(depth, 2 * units),
            down_w.T,
        ],
        [tokens, cotangent],
        seq,
        wide,
    )
    small_all = gathered[0].reshape(seq, 16, LANES).astype(jnp.float32)
    in_flat = gathered[1].reshape(width, 3 * chans)
    out_turned = gathered[2].reshape(width, chans)
    gu_flat = gathered[3].reshape(width, 2 * units)
    down_turned = gathered[4].reshape(width, units)
    gain_all = small_all[:, :2, :gain_cols].transpose(1, 0, 2).reshape(2, width)
    conv_taps = small_all[:, 2:5, :tap_cols].transpose(1, 0, 2).reshape(3, chans)
    inputs = whole_rows[0].reshape(group, width).astype(jnp.float32)
    valid = (jnp.arange(group, dtype=jnp.int32) < count)[:, None]
    grad_all = whole_rows[1].reshape(group, width)
    grad_all = jnp.where(valid, grad_all, jnp.zeros_like(grad_all))

    def own(value):
        return lax.dynamic_slice_in_dim(value, mp_place * rows, rows, 0)

    scale_one = norm_scale(inputs)
    mixer_all = (inputs * scale_one * gain_all[0]).astype(jnp.bfloat16)
    proj = jnp.dot(mixer_all, in_flat, preferred_element_type=jnp.float32)
    bgate = proj[:, :chans]
    cgate = proj[:, chans : 2 * chans]
    xin = proj[:, 2 * chans :]
    gated = (bgate * xin).astype(jnp.bfloat16)
    tail = lax.dynamic_slice_in_dim(gated, count - 2, 2, 0)
    before = from_behind(tail, "seq", 1)
    extended = jnp.concatenate([before, gated], axis=0).astype(jnp.float32)
    one_back = extended[1 : group + 1]
    two_back = extended[:group]
    keep_one = (positions >= 1).astype(jnp.float32)[:, None]
    keep_two = (positions >= 2).astype(jnp.float32)[:, None]
    current = gated.astype(jnp.float32)
    conv = (
        conv_taps[2] * current
        + keep_one * conv_taps[1] * one_back
        + keep_two * conv_taps[0] * two_back
    )
    mixed_in = (cgate * conv).astype(jnp.bfloat16)
    resid = inputs + mp_sum(contract_cols(mixed_in, out_turned))
    scale_two = norm_scale(resid)
    ff_all = (resid * scale_two * gain_all[1]).astype(jnp.bfloat16)
    both = jnp.dot(ff_all, gu_flat, preferred_element_type=jnp.float32)
    gate = both[:, :units]
    upper = both[:, units:]
    sigma = jax.nn.sigmoid(gate)
    active = gate * sigma
    hidden = (active * upper).astype(jnp.bfloat16)
    final = own(resid) + mp_sum_own(contract_cols(hidden, down_turned), rows)
    mixed = jnp.where(own(valid), final, jnp.zeros_like(final)).astype(jnp.bfloat16)

    grad_hidden = jnp.dot(grad_all, down_turned, preferred_element_type=jnp.float32)
    slope = sigma * (1.0 + gate * (1.0 - sigma))
    grad_both = jnp.concatenate([grad_hidden * upper * slope, grad_hidden * active], axis=1).astype(
        jnp.bfloat16
    )
    term_down = contract_rows(grad_all, hidden).astype(jnp.bfloat16)
    term_gu = contract_rows(ff_all, grad_both).astype(jnp.bfloat16)
    partial_two = contract_cols(grad_both, gu_flat)
    if wide == 2 and seq == DEPTH * 2 * CORES:
        row_ids = jnp.arange(group, dtype=jnp.int32)[:, None]
        masks = jnp.concatenate(
            [
                keep_one,
                keep_two,
                (row_ids == count - 2).astype(jnp.float32),
                (row_ids == count - 1).astype(jnp.float32),
            ],
            axis=1,
        )
        sum_gu, sum_down, sum_out, sum_in, grad_input, small_sums = mixer_back(
            term_gu,
            term_down,
            [
                partial_two.astype(jnp.bfloat16),
                partial_two,
                resid,
                grad_all,
                whole_rows[0].reshape(group, width),
                mixer_all,
                mixed_in,
                conv,
                cgate,
                xin,
                bgate,
                gated,
                one_back,
                two_back,
                masks,
                out_turned,
                in_flat,
                gain_all,
                conv_taps,
            ],
            seq,
        )
        here = lax.axis_index("seq")
        gain_size = gains.shape[1]
        return (
            mixed,
            grad_input,
            lax.dynamic_slice(small_sums, (0, (here * wide + mp_place) * gain_size), (2, gain_size)),
            sum_in.reshape(depth, 3, chans),
            sum_out.T,
            sum_gu.reshape(depth, 2, units),
            sum_down.T,
            lax.dynamic_slice(small_sums, (2, here * tap_cols), (3, tap_cols)),
        )
    back_two = mp_sum(partial_two)
    grad_resid = grad_all.astype(jnp.float32) + norm_back(resid, scale_two, gain_all[1], back_two)
    gain_two = jnp.sum(own(back_two * resid * scale_two), axis=0)
    grad_o_all = grad_resid.astype(jnp.bfloat16)
    term_out = contract_rows(grad_o_all, mixed_in).astype(jnp.bfloat16)
    grad_mix = jnp.dot(grad_o_all, out_turned, preferred_element_type=jnp.float32)
    grad_cgate = grad_mix * conv
    grad_conv = grad_mix * cgate
    lead_one = keep_one * grad_conv
    lead_two = keep_two * grad_conv
    head = jnp.stack(
        [conv_taps[0] * lead_two[0], conv_taps[1] * lead_one[0] + conv_taps[0] * lead_two[1]]
    )
    after = from_behind(head, "seq", -1)
    zero_one = jnp.zeros((1, chans), jnp.float32)
    zero_two = jnp.zeros((2, chans), jnp.float32)
    row_ids = jnp.arange(group, dtype=jnp.int32)[:, None]
    border = jnp.where(row_ids == count - 2, after[:1], jnp.where(row_ids == count - 1, after[1:], 0.0))
    grad_gated = (
        conv_taps[2] * grad_conv
        + conv_taps[1] * jnp.concatenate([lead_one[1:], zero_one], axis=0)
        + conv_taps[0] * jnp.concatenate([lead_two[2:], zero_two], axis=0)
        + border
    )
    term_conv = jnp.stack(
        [
            jnp.sum(lead_two * two_back, axis=0),
            jnp.sum(lead_one * one_back, axis=0),
            jnp.sum(grad_conv * current, axis=0),
        ]
    )
    grad_proj = jnp.concatenate([grad_gated * xin, grad_cgate, grad_gated * bgate], axis=1).astype(
        jnp.bfloat16
    )
    term_in = contract_rows(mixer_all, grad_proj).astype(jnp.bfloat16)
    back_one = mp_sum_own(contract_cols(grad_proj, in_flat), rows)
    own_inputs = own(inputs)
    own_scale = own(scale_one)
    grad_input = (
        own(grad_resid) + norm_back(own_inputs, own_scale, gain_all[0], back_one)
    ).astype(jnp.bfloat16)
    gain_one = jnp.sum(back_one * own_inputs * own_scale, axis=0)
    gain_terms = jnp.stack([gain_one, gain_two]).reshape(2, seq, gain_cols).transpose(1, 0, 2)
    tap_terms = term_conv.reshape(3, seq, tap_cols).transpose(1, 0, 2)
    small_terms = jnp.zeros((seq, 8, LANES), jnp.float32)
    small_terms = small_terms.at[:, :2, :gain_cols].set(gain_terms)
    small_terms = small_terms.at[:, 2:5, :tap_cols].set(tap_terms)
    sum_gu, sum_down, sum_out, sum_in, sum_small = scatter_all(
        [term_gu, term_down, term_out, term_in, small_terms.reshape(seq * 8, LANES)], seq
    )
    grad_gains = lax.psum_scatter(
        sum_small[:2, :gain_cols], "mp", scatter_dimension=1, tiled=True
    ) if wide != 2 else gain_share(sum_small[:2, :gain_cols], mp_place)
    return (
        mixed,
        grad_input,
        grad_gains,
        sum_in.reshape(depth, 3, chans),
        sum_out.T,
        sum_gu.reshape(depth, 2, units),
        sum_down.T,
        sum_small[2:5, :tap_cols],
    )


def gain_share(sums, place):
    cols = sums.shape[1] // 2
    total = sums + lax.ppermute(sums, "mp", [(0, 1), (1, 0)])
    return lax.dynamic_slice_in_dim(total, place * cols, cols, 1)


def solution(mesh):
    placed = (
        P(("seq", "mp"), None),
        P("seq"),
        P("seq"),
        P(("seq", "mp"), None),
        P(None, ("seq", "mp")),
        P("seq", None, "mp"),
        P("mp", "seq"),
        P("seq", None, "mp"),
        P("mp", "seq"),
        P(None, ("mp", "seq")),
    )
    return jax.shard_map(
        on_device,
        mesh=mesh,
        in_specs=placed,
        out_specs=(
            P(("seq", "mp"), None),
            P(("seq", "mp"), None),
            P(None, ("seq", "mp")),
            P("seq", None, "mp"),
            P("mp", "seq"),
            P("seq", None, "mp"),
            P("mp", "seq"),
            P(None, ("mp", "seq")),
        ),
        check_vma=False,
    )
```
